32 devices in a mesh: dp: 8 (over z, x), tensor: 4 (over y, core).
Axes of the slice: x: 2, y: 2, z: 4, core: 2. Of those that a mesh axis runs over, the one named last changes fastest.
Arguments:
- tokens: bfloat16 [2048, 4096], P('dp', 'tensor'), may hold values from -6 to 6
- out_grad: bfloat16 [2048, 4096], P('dp', 'tensor'), may hold values from -0.59765625 to 0.59765625
- w_in: bfloat16 [96, 128, 128], P('tensor'), may hold values from -0.25 to 0.25
- w_out: bfloat16 [96, 128, 128], P('tensor'), may hold values from -0.25 to 0.25
- block_rows: int32 [4, 24], P('tensor'), may hold values from -1 to 31, as said below
- block_cols: int32 [4, 24], P('tensor'), may hold values from -1 to 27, as said below
Outputs:
- in_grad: bfloat16 [2048, 4096], P('dp')
- win_grad: float32 [96, 16384], P('tensor', 'dp')
- wout_grad: float32 [96, 16384], P('tensor', 'dp')
The draws below stay inside these ranges and needn't reach their ends.
Inputs may be any that keep to these rules, and one draw needn't show every extreme that they name: `block_rows`: -1 marks an empty slot; the live slots of one tensor index name distinct blocks; at least 12 slots of each tensor index are live, and all 24 slots of some tensor index are live. `block_cols`: -1 exactly where block_rows is -1.
All inputs are finite; a program needn't handle non-finite values.
Results may differ from the reference program's by a relative error of at most 0.02.
Values may be sent and summed in bfloat16 or wider, within the bound.
A program may use at most 64 MiB of HBM per device.

```python
import jax
import jax.numpy as jnp
from jax import lax

D = 4096
BLK = 128
TOK_DEV = 256
CAP = 24
TOKENS = 2048
ROWBLK = 32
HID_DEV = 28
SLOTS = 96
N_DP = 8
N_TENSOR = 4


def shared_layout(key):
    base = jax.random.fold_in(key, 7)
    key_full, key_count, key_place, key_order = jax.random.split(base, 4)
    full_index = jax.random.randint(key_full, (), 0, N_TENSOR)
    counts = jax.random.randint(key_count, (N_TENSOR,), CAP // 2, CAP + 1)
    counts = jnp.where(jnp.arange(N_TENSOR) == full_index, CAP, counts)
    place_keys = jax.random.split(key_place, N_TENSOR)
    order_keys = jax.random.split(key_order, N_TENSOR)
    places = jax.vmap(lambda k: jax.random.permutation(k, ROWBLK * HID_DEV)[:CAP])(place_keys)
    ranks = jax.vmap(lambda k: jax.random.permutation(k, CAP))(order_keys)
    live = ranks < counts[:, None]
    rows = jnp.where(live, places // HID_DEV, -1).astype(jnp.int32)
    cols = jnp.where(live, places % HID_DEV, -1).astype(jnp.int32)
    return (rows, cols)


def draw_block_rows(key, part):
    return shared_layout(key)[0]


def draw_block_cols(key, part):
    return shared_layout(key)[1]


def level_of(rng, extent, cuts, low, high):
    factor_of = 1.0
    for dim, blocks in cuts:
        draws = jax.random.uniform(jax.random.fold_in(jax.random.fold_in(rng, 6), dim), (blocks,), jnp.float32, low / len(cuts), high / len(cuts))
        factor_of = factor_of * jnp.repeat(jnp.exp(draws), extent[dim] // blocks).reshape((-1,) + (1,) * (len(extent) - 1 - dim))
    return factor_of


def noise(rng, shape, width, reach, shards=(), kind=jnp.bfloat16):
    values = jax.random.normal(rng, shape, jnp.float32) * width
    if len(shards) > 0:
        values = level_of(rng, shape, shards, -0.22, 0.18) * values
    return jnp.clip(values, min=-reach, max=reach).astype(kind)


def setup_inputs(seed: int = 0) -> dict:
    keys = jax.random.split(jax.random.key(seed), 7)
    return {
        "tokens": noise(keys[0], (TOKENS, D), 1.0, 6.0, ((0, 8), (1, 4))),
        "out_grad": noise(keys[1], (TOKENS, D), 0.1, 0.59765625, ((0, 8), (1, 4))),
        "w_in": noise(keys[2], (SLOTS, BLK, BLK), (4 * BLK) ** -0.5, 0.25, ((0, 4),)),
        "w_out": noise(keys[3], (SLOTS, BLK, BLK), (4 * BLK) ** -0.5, 0.25, ((0, 4),)),
        "block_rows": draw_block_rows(jax.random.fold_in(keys[6], 71), 0),
        "block_cols": draw_block_cols(jax.random.fold_in(keys[6], 71), 0),
    }


highest = lax.Precision.HIGHEST
clip_limit = 4.0


def device_pass(tokens_now, cotangent, w_in, w_out, block_rows, block_cols, bin_scale):
    rows = block_rows.reshape(-1)
    cols = block_cols.reshape(-1)
    live = rows >= 0
    livef = live.astype(jnp.float32)
    shard_of = (jnp.arange(rows.shape[0], dtype=jnp.int32) // CAP).astype(jnp.int32)
    global_col = jnp.where(live, shard_of * HID_DEV + cols, 0).astype(jnp.int32)
    safe_rows = jnp.where(live, rows, 0).astype(jnp.int32)
    col_hot = (global_col[:, None] == jnp.arange(HID_DEV * N_TENSOR, dtype=jnp.int32)[None, :]).astype(jnp.float32) * livef[:, None]
    row_hot = (safe_rows[:, None] == jnp.arange(ROWBLK, dtype=jnp.int32)[None, :]).astype(jnp.float32) * livef[:, None]
    in_blocks = tokens_now.reshape(TOK_DEV, ROWBLK, BLK).transpose(1, 0, 2)
    grad_blocks = cotangent.reshape(TOK_DEV, ROWBLK, BLK).transpose(1, 0, 2)
    picked = jnp.take(in_blocks, safe_rows, axis=0).astype(jnp.float32)
    picked_grad = jnp.take(grad_blocks, safe_rows, axis=0).astype(jnp.float32)
    win_wide = w_in.astype(jnp.float32)
    wout_wide = w_out.astype(jnp.float32)
    pre = jnp.einsum('sc,sth->cth', col_hot, jnp.einsum('stk,skh->sth', picked, win_wide), precision=highest)
    hidden = jax.nn.silu(pre).astype(jnp.bfloat16)
    dhidden = jnp.einsum('sc,sth->cth', col_hot, jnp.einsum('std,shd->sth', picked_grad, wout_wide), precision=highest)
    sigma = jax.nn.sigmoid(pre)
    dpre = (dhidden * sigma * (1.0 + pre * (1.0 - sigma))).astype(jnp.bfloat16)
    dpre_picked = jnp.take(dpre, global_col, axis=0).astype(jnp.float32)
    hidden_picked = jnp.take(hidden, global_col, axis=0).astype(jnp.float32)
    slot_terms = jnp.einsum('sth,sdh->std', dpre_picked, win_wide)

    def shard_part(total, index):
        hot_now = lax.dynamic_slice_in_dim(row_hot, index * CAP, CAP, 0)
        terms_now = lax.dynamic_slice_in_dim(slot_terms, index * CAP, CAP, 0)
        part = jnp.einsum('sr,std->rtd', hot_now, terms_now, precision=highest)
        part = lax.optimization_barrier(part.astype(jnp.bfloat16))
        return total + part.astype(jnp.float32), None

    zero_grad = jnp.zeros((ROWBLK, TOK_DEV, BLK), jnp.float32)
    in_grad, unused = lax.scan(shard_part, zero_grad, jnp.arange(N_TENSOR, dtype=jnp.int32))
    in_grad = in_grad.transpose(1, 0, 2).reshape(TOK_DEV, D).astype(jnp.bfloat16)
    grad_in = jnp.einsum('stk,sth->skh', picked, dpre_picked) * livef[:, None, None]
    grad_out = jnp.einsum('sth,std->shd', hidden_picked, picked_grad) * livef[:, None, None]
    bins_in = jnp.floor(jnp.clip(grad_in, -clip_limit, clip_limit) * bin_scale)
    bins_out = jnp.floor(jnp.clip(grad_out, -clip_limit, clip_limit) * bin_scale)
    return in_grad, bins_in, bins_out


def reference(tokens, out_grad, w_in, w_out, block_rows, block_cols):
    bin_scale = 4194304.0 / N_DP
    token_sets = tokens.reshape(N_DP, TOK_DEV, D)
    grad_sets = out_grad.reshape(N_DP, TOK_DEV, D)

    def advance(carry, pair):
        in_grad, bins_in, bins_out = device_pass(pair[0], pair[1], w_in, w_out, block_rows, block_cols, bin_scale)
        return (carry[0] + bins_in, carry[1] + bins_out), in_grad

    zeros = jnp.zeros((N_TENSOR * CAP, BLK, BLK), jnp.float32)
    (total_in, total_out), grads = lax.scan(advance, (zeros, zeros), (token_sets, grad_sets))
    in_grad = grads.reshape(TOKENS, D)
    win_grad = (total_in / bin_scale).reshape(N_TENSOR * CAP, BLK * BLK)
    wout_grad = (total_out / bin_scale).reshape(N_TENSOR * CAP, BLK * BLK)
    return in_grad, win_grad, wout_grad
```

```python
import functools

import jax
import jax.numpy as jnp
from jax import lax
from jax.experimental import pallas as pl
from jax.experimental.pallas import tpu as pltpu
from jax.sharding import PartitionSpec as P

MESH = pl.DeviceIdType.MESH
BF, F32, I32 = jnp.bfloat16, jnp.float32, jnp.int32
CLIP = 4.0
UNROLL = 4


def dot(a, b, ca, cb):
    return lax.dot_general(a, b, (((ca,), (cb,)), ((), ())), preferred_element_type=F32)


def order_of(key, idx):
    equal = key[None, :] == key[:, None]
    earlier = idx[None, :] < idx[:, None]
    rank = jnp.sum(((key[None, :] < key[:, None]) | (equal & earlier)).astype(I32), 1)
    hot = rank[None, :] == idx[:, None]
    perm = jnp.sum(jnp.where(hot, idx[None, :], 0), 1)
    joins = jnp.any(equal & earlier, 1)
    same = jnp.sum(jnp.where(hot, joins[None, :].astype(I32), 0), 1)
    end = jnp.max(jnp.where(equal, rank[None, :], 0), 1)
    return rank, perm, same, end


def table(block_rows, block_cols, row_count):
    rows, cols = block_rows[0], block_cols[0]
    cap = rows.shape[0]
    idx = jnp.arange(cap, dtype=I32)
    live = rows >= 0
    _, perm_c, same_c, end_c = order_of(jnp.where(live, cols, (1 << 20) + idx), idx)
    rank_r, perm_r, same_r, _ = order_of(jnp.where(live, rows, (1 << 20) + idx), idx)
    safe = jnp.where(live, rows, 0)
    row_c = jnp.sum(jnp.where(perm_c[:, None] == idx[None, :], safe[None, :], 0), 1)
    hit = rows[None, :] == jnp.arange(row_count, dtype=I32)[:, None]
    last_r = jnp.max(jnp.where(hit, rank_r[None, :], 0), 1)
    has_r = jnp.any(hit, 1).astype(I32)
    lines = [
        perm_c,
        same_c,
        end_c,
        safe,
        row_c,
        live.astype(I32),
        perm_r,
        same_r,
        last_r,
        has_r,
    ]
    size = max(cap, row_count)
    return jnp.stack([jnp.pad(v, (0, size - v.shape[0])) for v in lines])


def kernel(
    n_dp, n_t,
    meta, tok_hbm, grad_hbm, win_hbm, wout_hbm,
    dx_out, gin_out, gout_out,
    tok0, tok1, grad0, grad1, tcut0, tcut1, gcut0, gcut1, win, wout, scan_p, scan_h, terms, rscan, hid, dpre,
    part, rsib, ysum, yrecv, res, stage_i, stage_o, xr_i, xr_o, zs_i, zs_o, zr_i, zr_o,
    ag_send, ag_recv, sib_send, sib_recv, loc, wloc, p_send, p_recv, r_send, r_recv,
    o_send, o_recv, o_loc, x_send, x_recv, z_send, z_recv,
):
    tok, grad = (tok0, tok1), (grad0, grad1)
    cap, side = win.shape[0], win.shape[1]
    half = tok0.shape[1]
    n_y, n_j = n_t // 2, n_dp // 2
    row_count = n_t * tok0.shape[2] // side
    span = side // n_dp
    wide = row_count * side // 2
    scale = 4194304.0 / n_dp
    d, t = lax.axis_index("dp"), lax.axis_index("tensor")
    c, y = lax.rem(t, 2), t // 2
    sib = y * 2 + (1 - c)
    b, j = lax.rem(d, 2), d // 2
    xpeer = j * 2 + (1 - b)

    def y_at(k):
        return lax.rem(y + k + n_y, n_y) * 2 + c

    def j_at(k):
        return lax.rem(j + k + n_j, n_j)

    barrier = pltpu.get_barrier_semaphore()
    peers = [{"tensor": sib}, {"dp": xpeer}]
    peers += [{"tensor": y_at(k)} for k in range(1, n_y)]
    peers += [{"dp": j_at(k) * 2 + b} for k in range(1, n_j)]
    for peer in peers:
        pl.semaphore_signal(barrier, inc=1, device_id=peer, device_id_type=MESH)

    def remote(src, dst, ss, rs, peer):
        return pltpu.make_async_remote_copy(
            src_ref=src, dst_ref=dst, send_sem=ss, recv_sem=rs, device_id=peer, device_id_type=MESH
        )

    hbm = (tok_hbm, grad_hbm)
    held = (tok, grad)
    cut = ((tcut0, tcut1), (gcut0, gcut1))

    def shard(a, h):
        return hbm[a].at[pl.ds(h * half, half), :]

    def ag_y(a, h, k):
        return remote(shard(a, h), held[a][h].at[t], ag_send.at[a, h, k - 1],
                      ag_recv.at[a, h, k - 1], {"tensor": y_at(k)})

    def ag_sib(a, h, k):
        src_t = y_at(-k)
        src = shard(a, h) if k == 0 else held[a][h].at[src_t]
        return remote(src, held[a][h].at[src_t], sib_send.at[a, h, k],
                      sib_recv.at[a, h, k], {"tensor": sib})

    def own(a, h):
        return pltpu.make_async_copy(shard(a, h), held[a][h].at[t], loc.at[a, h])

    weights = [pltpu.make_async_copy(win_hbm, win, wloc.at[0]),
               pltpu.make_async_copy(wout_hbm, wout, wloc.at[1])]

    def start_y(a, h):
        for k in range(1, n_y):
            ag_y(a, h, k).start()

    def pass_on(a, h):
        for k in range(1, n_y):
            ag_y(a, h, k).wait_recv()
            ag_sib(a, h, k).start()

    def settle(h):
        for a in range(2):
            own(a, h).wait()
            for k in range(n_y):
                ag_sib(a, h, k).wait_recv()

    for w in weights:
        w.start()
    for a in range(2):
        for h in range(2):
            own(a, h).start()
    pl.semaphore_wait(barrier, len(peers))
    start_y(0, 0)
    start_y(1, 0)
    for h in range(2):
        for a in range(2):
            ag_sib(a, h, 0).start()

    def split(h):
        per = tok0.shape[2] // side
        for a in range(2):
            def body(g, carry):
                for u in range(per):
                    cut[a][h][g * per + u] = held[a][h][g, :, u * side:(u + 1) * side]
                return carry
            lax.fori_loop(0, n_t, body, 0)

    def loop(count, body, carry):
        def outer(g, carry):
            for u in range(UNROLL):
                carry = body(g * UNROLL + u, carry)
            return carry
        return lax.fori_loop(0, count // UNROLL, outer, carry)

    def forward(h):
        def body(i, carry):
            acc_p, acc_h = carry
            s = meta[0, i]
            keep = meta[1, i].astype(F32)
            row = meta[4, i]
            acc_p = acc_p * keep + dot(cut[0][h][row], win[s], 1, 0)
            acc_h = acc_h * keep + dot(cut[1][h][row], wout[s], 1, 1)
            scan_p[i] = acc_p
            scan_h[i] = acc_h
            return acc_p, acc_h
        zero = jnp.zeros((half, side), F32)
        loop(cap, body, (zero, zero))

        def point(s, carry):
            e = meta[2, s]
            pre, dh = scan_p[e], scan_h[e]
            sigma = 1.0 / (1.0 + jnp.exp(-pre))
            hid[s, pl.ds(h * half, half), :] = (pre * sigma).astype(BF)
            dpre[s, pl.ds(h * half, half), :] = (
                dh * sigma * (1.0 + pre * (1.0 - sigma))
            ).astype(BF)
            return carry
        loop(cap, point, 0)

    def back(h):
        def term(s, carry):
            terms[s] = dot(dpre[s, pl.ds(h * half, half), :], win[s], 1, 1)
            return carry
        loop(cap, term, 0)

        def body(i, acc):
            acc = acc * meta[7, i].astype(F32) + terms[meta[6, i]]
            rscan[i] = acc
            return acc
        loop(cap, body, jnp.zeros((half, side), F32))
        for r in range(row_count):
            at, off = divmod(r * side, wide)
            part[h, at, :, pl.ds(off, side)] = (
                rscan[meta[8, r]] * meta[9, r].astype(F32)
            ).astype(BF)

    def exchange(h):
        return remote(part.at[h, 1 - c], rsib.at[h], p_send.at[h], p_recv.at[h], {"tensor": sib})

    def ring(h, k):
        return remote(ysum.at[h], yrecv.at[h, y], r_send.at[h, k - 1], r_recv.at[h, k - 1],
                      {"tensor": y_at(k)})

    def y_out(h):
        exchange(h).wait_recv()

        def rows(i, carry):
            at = pl.ds(pl.multiple_of(i * 16, 16), 16)
            ysum[h, at, :] = (
                part[h, c, at, :].astype(F32) + rsib[h, at, :].astype(F32)
            ).astype(BF)
            return carry
        lax.fori_loop(0, half // 16, rows, 0)
        for k in range(1, n_y):
            ring(h, k).start()

    def out_at(h):
        return dx_out.at[pl.ds(h * half, half), pl.ds(pl.multiple_of(c * wide, side), wide)]

    def out_sib(h):
        return remote(res.at[h], out_at(h), o_send.at[h], o_recv.at[h], {"tensor": sib})

    def out_own(h):
        return pltpu.make_async_copy(res.at[h], out_at(h), o_loc.at[h])

    def y_in(h):
        for k in range(1, n_y):
            ring(h, k).wait_recv()

        def rows(i, carry):
            at = pl.ds(pl.multiple_of(i * 16, 16), 16)
            mine = ysum[h, at, :].astype(F32)
            acc = jnp.zeros_like(mine)
            for g in range(n_y):
                acc = acc + jnp.where(y == g, mine, yrecv[h, g, at, :].astype(F32))
            res[h, at, :] = acc.astype(BF)
            return carry
        lax.fori_loop(0, half // 16, rows, 0)
        out_sib(h).start()
        out_own(h).start()

    stage, xr, zs, zr = (stage_i, stage_o), (xr_i, xr_o), (zs_i, zs_o), (zr_i, zr_o)
    g_out = (gin_out, gout_out)

    def wgrad(kind):
        def body(s, carry):
            row = meta[3, s]
            block = jnp.concatenate([cut[kind][0][row], cut[kind][1][row]], 0)
            g = dot(block, dpre[s], 0, 0) if kind == 0 else dot(hid[s], block, 0, 0)
            q = jnp.floor(jnp.clip(g, -CLIP, CLIP) * scale) * meta[5, s].astype(F32)
            q = q.astype(BF)
            for p in range(n_dp):
                stage[kind][p % 2, p // 2, s] = q[p * span:(p + 1) * span]
            return carry
        loop(cap, body, 0)

    def x_swap(kind):
        return remote(stage[kind].at[1 - b], xr[kind], x_send.at[kind], x_recv.at[kind],
                      {"dp": xpeer})

    def z_send_to(kind, k):
        return remote(zs[kind].at[j_at(k)], zr[kind].at[k - 1], z_send.at[kind, k - 1],
                      z_recv.at[kind, k - 1], {"dp": j_at(k) * 2 + b})

    def z_out(kind):
        x_swap(kind).wait_recv()
        for k in list(range(1, n_j)) + [0]:
            g = j_at(k)
            zs[kind][g] = (stage[kind][b, g].astype(F32) + xr[kind][g].astype(F32)).astype(BF)
            if k:
                z_send_to(kind, k).start()

    def z_in(kind):
        acc = zs[kind][j].astype(F32)
        for k in range(1, n_j):
            z_send_to(kind, k).wait_recv()
            acc = acc + zr[kind][k - 1].astype(F32)
        g_out[kind][...] = acc * (1.0 / scale)

    pass_on(0, 0)
    start_y(0, 1)
    pass_on(1, 0)
    start_y(1, 1)
    for w in weights:
        w.wait()
    settle(0)
    split(0)
    forward(0)
    back(0)
    exchange(0).start()
    y_out(0)
    pass_on(0, 1)
    pass_on(1, 1)
    settle(1)
    split(1)
    forward(1)
    wgrad(1)
    x_swap(1).start()
    wgrad(0)
    x_swap(0).start()
    back(1)
    exchange(1).start()
    y_out(1)
    z_out(1)
    z_out(0)
    y_in(0)
    z_in(1)
    y_in(1)
    z_in(0)
    for h in range(2):
        out_own(h).wait()
        out_sib(h).wait()
        exchange(h).wait_send()
        for a in range(2):
            for k in range(1, n_y):
                ag_y(a, h, k).wait_send()
            for k in range(n_y):
                ag_sib(a, h, k).wait_send()
        for k in range(1, n_y):
            ring(h, k).wait_send()
    for kind in range(2):
        x_swap(kind).wait_send()
        for k in range(1, n_j):
            z_send_to(kind, k).wait_send()


def local(n_dp, n_t, tokens, out_grad, w_in, w_out, block_rows, block_cols):
    tok_count, shard_width = tokens.shape
    cap, side = w_in.shape[0], w_in.shape[1]
    width = shard_width * n_t
    half, wide, span = tok_count // 2, width // 2, side // n_dp
    n_y, n_j = n_t // 2, n_dp // 2
    meta = table(block_rows, block_cols, width // side)
    vm = pltpu.VMEM
    dma = pltpu.SemaphoreType.DMA
    gathered = vm((n_t, half, shard_width), BF)
    cuts = vm((width // side, half, side), BF)
    blocks = vm((cap, side, side), BF)
    slots = vm((cap, half, side), F32)
    stage = vm((2, n_j, cap, span, side), BF)
    piece = vm((n_j, cap, span, side), BF)
    landing = vm((max(n_j - 1, 1), cap, span, side), BF)
    scratch = [
        gathered, gathered, gathered, gathered, cuts, cuts, cuts, cuts, blocks, blocks, slots, slots, slots, slots,
        vm((cap, tok_count, side), BF), vm((cap, tok_count, side), BF),
        vm((2, 2, half, wide), BF), vm((2, half, wide), BF), vm((2, half, wide), BF),
        vm((2, n_y, half, wide), BF), vm((2, half, wide), BF),
        stage, stage, piece, piece, piece, piece, landing, landing,
        dma((2, 2, n_y - 1)), dma((2, 2, n_y - 1)), dma((2, 2, n_y)), dma((2, 2, n_y)),
        dma((2, 2)), dma((2,)), dma((2,)), dma((2,)), dma((2, n_y - 1)), dma((2, n_y - 1)),
        dma((2,)), dma((2,)), dma((2,)), dma((2,)), dma((2,)),
        dma((2, n_j - 1)), dma((2, n_j - 1)),
    ]
    any_space = pl.BlockSpec(memory_space=pl.ANY)
    grads = jax.ShapeDtypeStruct((cap, span, side), F32)
    in_grad, win_grad, wout_grad = pl.pallas_call(
        functools.partial(kernel, n_dp, n_t),
        out_shape=(jax.ShapeDtypeStruct((tok_count, width), BF), grads, grads),
        in_specs=[pl.BlockSpec(memory_space=pltpu.SMEM)] + [any_space] * 4,
        out_specs=(any_space, pl.BlockSpec(memory_space=vm), pl.BlockSpec(memory_space=vm)),
        scratch_shapes=scratch,
        compiler_params=pltpu.CompilerParams(
            collective_id=0, has_side_effects=True, vmem_limit_bytes=56 * 1024 * 1024
        ),
        cost_estimate=pl.CostEstimate(
            flops=10 * cap * tok_count * side * side,
            bytes_accessed=8 * tok_count * width,
            transcendentals=cap * tok_count * side,
        ),
    )(meta, tokens, out_grad, w_in, w_out)
    return in_grad, win_grad.reshape(cap, span * side), wout_grad.reshape(cap, span * side)


def solution(mesh):
    in_specs = (
        P("dp", "tensor"),
        P("dp", "tensor"),
        P("tensor", None, None),
        P("tensor", None, None),
        P("tensor", None),
        P("tensor", None),
    )
    out_specs = (P("dp", None), P("tensor", "dp"), P("tensor", "dp"))
    body = functools.partial(local, mesh.shape["dp"], mesh.shape["tensor"])
    return jax.shard_map(body, mesh=mesh, in_specs=in_specs, out_specs=out_specs, check_vma=False)
```

```python
import functools

import jax
import jax.numpy as jnp
from jax import lax
from jax.experimental import pallas as pl
from jax.experimental.pallas import tpu as pltpu
from jax.sharding import PartitionSpec as P

MESH = pl.DeviceIdType.MESH
BF, F32, I32 = jnp.bfloat16, jnp.float32, jnp.int32
CLIP = 4.0
UNROLL = 4
PREV_COL, END_COL, ROW, LIVE, PREV_ROW, LAST = range(6)


def dot(a, b, ca, cb):
    return lax.dot_general(a, b, (((ca,), (cb,)), ((), ())), preferred_element_type=F32)


def loop(count, body):
    def outer(g, carry):
        for u in range(UNROLL):
            body(g * UNROLL + u)
        return carry

    lax.fori_loop(0, count // UNROLL, outer, 0)


def kernel(
    n_dp, n_t, chunk,
    rows, cols, tok_hbm, grad_hbm, win_hbm, wout_hbm,
    dx_out, gin_out, gout_out,
    table, tok0, tok1, grad0, grad1, tcut, gcut0, gcut1, win, wout, scan_p, scan_h, rscan,
    hid, gate, dpre, part, rsib, ysum, yrecv, res, stage, xr, zs, zr,
    ag_send, ag_recv, sib_send, sib_recv, loc, wloc, p_send, p_recv, r_send, r_recv,
    o_send, o_recv, o_loc, x_send, x_recv, z_send, z_recv,
):
    cap, side = win.shape[0], win.shape[1]
    half = tok0.shape[1]
    per = tok0.shape[2] // side
    n_y, n_j, n_c = n_t // 2, n_dp // 2, cap // chunk
    row_count = n_t * per
    span = side // n_dp
    wide = row_count * side // 2
    scale = 4194304.0 / n_dp
    d, t = lax.axis_index("dp"), lax.axis_index("tensor")
    c, y = lax.rem(t, 2), t // 2
    sib = y * 2 + (1 - c)
    b, j = lax.rem(d, 2), d // 2
    xpeer = j * 2 + (1 - b)

    def y_at(k):
        return lax.rem(y + k + n_y, n_y) * 2 + c

    def j_at(k):
        return lax.rem(j + k + n_j, n_j)

    barrier = pltpu.get_barrier_semaphore()
    peers = [{"tensor": sib}, {"dp": xpeer}]
    peers += [{"tensor": y_at(k)} for k in range(1, n_y)]
    peers += [{"dp": j_at(k) * 2 + b} for k in range(1, n_j)]
    for peer in peers:
        pl.semaphore_signal(barrier, inc=1, device_id=peer, device_id_type=MESH)

    def remote(src, dst, ss, rs, peer):
        return pltpu.make_async_remote_copy(
            src_ref=src, dst_ref=dst, send_sem=ss, recv_sem=rs, device_id=peer, device_id_type=MESH
        )

    hbm = (tok_hbm, grad_hbm)
    held = ((tok0, tok1), (grad0, grad1))

    def shard(a, h):
        return hbm[a].at[pl.ds(h * half, half), :]

    def ag_y(a, h, k):
        return remote(shard(a, h), held[a][h].at[t], ag_send.at[a, h, k - 1],
                      ag_recv.at[a, h, k - 1], {"tensor": y_at(k)})

    def ag_sib(a, h, k):
        src_t = y_at(-k)
        src = shard(a, h) if k == 0 else held[a][h].at[src_t]
        return remote(src, held[a][h].at[src_t], sib_send.at[a, h, k],
                      sib_recv.at[a, h, k], {"tensor": sib})

    def own(a, h):
        return pltpu.make_async_copy(shard(a, h), held[a][h].at[t], loc.at[a, h])

    weights = [pltpu.make_async_copy(win_hbm, win, wloc.at[0]),
               pltpu.make_async_copy(wout_hbm, wout, wloc.at[1])]

    def start_y(a, h):
        for k in range(1, n_y):
            ag_y(a, h, k).start()

    def pass_on(a, h):
        for k in range(1, n_y):
            ag_y(a, h, k).wait_recv()
            ag_sib(a, h, k).start()

    def settle(a, h):
        own(a, h).wait()
        for k in range(n_y):
            ag_sib(a, h, k).wait_recv()

        def split(g, carry):
            for u in range(per):
                block = held[a][h][g, :, u * side:(u + 1) * side]
                if a == 0:
                    tcut[g * per + u, h * half:(h + 1) * half, :] = block
                else:
                    (gcut0, gcut1)[h][g * per + u] = block
            return carry

        lax.fori_loop(0, n_t, split, 0)

    def tables():
        def of_slot(s, carry):
            col, row = cols[0, s], rows[0, s]
            prev_col, prev_row, end_col = I32(cap), I32(cap), I32(0)
            for q in range(cap):
                same_col, same_row = cols[0, q] == col, rows[0, q] == row
                prev_col = jnp.where(same_col & (q < s), q, prev_col)
                prev_row = jnp.where(same_row & (q < s), q, prev_row)
                end_col = jnp.where(same_col, q, end_col)
            table[PREV_COL, s] = prev_col
            table[PREV_ROW, s] = prev_row
            table[END_COL, s] = end_col
            table[ROW, s] = jnp.maximum(row, 0)
            table[LIVE, s] = jnp.where(row >= 0, 1, 0)
            return carry

        def of_row(r, carry):
            last = I32(cap)
            for q in range(cap):
                last = jnp.where(rows[0, q] == r, q, last)
            table[LAST, r] = last
            return carry

        lax.fori_loop(0, cap, of_slot, 0)
        lax.fori_loop(0, row_count, of_row, 0)

    def forward():
        def body(s):
            term = dot(tcut[table[ROW, s]], win[s], 1, 0)
            scan_p[s] = term + scan_p[table[PREV_COL, s]]

        loop(cap, body)

        def point(s):
            pre = scan_p[table[END_COL, s]]
            sigma = 1.0 / (1.0 + jnp.exp(-pre))
            hid[s] = (pre * sigma).astype(BF)
            gate[s] = sigma * (1.0 + pre * (1.0 - sigma))

        loop(cap, point)

    def backward(h):
        at = pl.ds(h * half, half)

        def body(s):
            term = dot((gcut0, gcut1)[h][table[ROW, s]], wout[s], 1, 1)
            scan_h[s] = term + scan_h[table[PREV_COL, s]]

        loop(cap, body)

        def point(s):
            dpre[s, at, :] = (scan_h[table[END_COL, s]] * gate[s, at, :]).astype(BF)

        loop(cap, point)

        def term(s):
            rscan[s] = dot(dpre[s, at, :], win[s], 1, 1) + rscan[table[PREV_ROW, s]]

        loop(cap, term)
        for r in range(row_count):
            at_half, off = divmod(r * side, wide)
            part[h, at_half, :, pl.ds(off, side)] = rscan[table[LAST, r]].astype(BF)

    def exchange(h):
        return remote(part.at[h, 1 - c], rsib.at[h], p_send.at[h], p_recv.at[h], {"tensor": sib})

    def ring(h, k):
        return remote(ysum.at[h], yrecv.at[h, y], r_send.at[h, k - 1], r_recv.at[h, k - 1],
                      {"tensor": y_at(k)})

    def y_out(h):
        exchange(h).wait_recv()

        def band(i, carry):
            at = pl.ds(pl.multiple_of(i * 16, 16), 16)
            ysum[h, at, :] = (
                part[h, c, at, :].astype(F32) + rsib[h, at, :].astype(F32)
            ).astype(BF)
            return carry

        lax.fori_loop(0, half // 16, band, 0)
        for k in range(1, n_y):
            ring(h, k).start()

    def out_at(h):
        return dx_out.at[pl.ds(h * half, half), pl.ds(pl.multiple_of(c * wide, side), wide)]

    def out_sib(h):
        return remote(res.at[h], out_at(h), o_send.at[h], o_recv.at[h], {"tensor": sib})

    def out_own(h):
        return pltpu.make_async_copy(res.at[h], out_at(h), o_loc.at[h])

    def y_in(h):
        for k in range(1, n_y):
            ring(h, k).wait_recv()

        def band(i, carry):
            at = pl.ds(pl.multiple_of(i * 16, 16), 16)
            mine = ysum[h, at, :].astype(F32)
            acc = jnp.zeros_like(mine)
            for g in range(n_y):
                acc = acc + jnp.where(y == g, mine, yrecv[h, g, at, :].astype(F32))
            res[h, at, :] = acc.astype(BF)
            return carry

        lax.fori_loop(0, half // 16, band, 0)
        out_sib(h).start()
        out_own(h).start()

    g_out = (gin_out, gout_out)

    def x_swap(kind, n):
        q = kind * n_c + n
        return remote(stage.at[q, 1 - b], xr.at[q], x_send.at[q], x_recv.at[q], {"dp": xpeer})

    def wgrad(kind, n):
        def body(i):
            s = n * chunk + i
            row = table[ROW, s]
            if kind == 0:
                g = dot(tcut[row], dpre[s], 0, 0)
            else:
                g = dot(hid[s], jnp.concatenate([gcut0[row], gcut1[row]], 0), 0, 0)
            bins = jnp.floor(jnp.clip(g, -CLIP, CLIP) * scale) * table[LIVE, s].astype(F32)
            bins = bins.astype(BF)
            for p in range(n_dp):
                stage[kind * n_c + n, p % 2, p // 2, i] = bins[p * span:(p + 1) * span]

        loop(chunk, body)
        x_swap(kind, n).start()

    def z_copy(kind, n, k):
        q = kind * n_c + n
        return remote(zs.at[q, j_at(k)], zr.at[q, k - 1], z_send.at[q, k - 1],
                      z_recv.at[q, k - 1], {"dp": j_at(k) * 2 + b})

    def z_out(kind, n):
        q = kind * n_c + n
        x_swap(kind, n).wait_recv()
        for k in list(range(1, n_j)) + [0]:
            g = j_at(k)
            zs[q, g] = (stage[q, b, g].astype(F32) + xr[q, g].astype(F32)).astype(BF)
            if k:
                z_copy(kind, n, k).start()

    def z_in(kind, n):
        q = kind * n_c + n
        acc = zs[q, j].astype(F32)
        for k in range(1, n_j):
            z_copy(kind, n, k).wait_recv()
            acc = acc + zr[q, k - 1].astype(F32)
        acc = acc * (1.0 / scale)
        for r in range(span):
            g_out[kind][n * chunk:(n + 1) * chunk, r * side:(r + 1) * side] = acc[:, r, :]

    for w in weights:
        w.start()
    for a in range(2):
        for h in range(2):
            own(a, h).start()
    pl.semaphore_wait(barrier, len(peers))
    start_y(0, 0)
    start_y(0, 1)
    for a in range(2):
        for h in range(2):
            ag_sib(a, h, 0).start()
    tables()
    scan_p[cap] = jnp.zeros(scan_p.shape[1:], F32)
    scan_h[cap] = jnp.zeros(scan_h.shape[1:], F32)
    rscan[cap] = jnp.zeros(rscan.shape[1:], F32)
    pass_on(0, 0)
    start_y(1, 0)
    pass_on(0, 1)
    start_y(1, 1)
    for w in weights:
        w.wait()
    settle(0, 0)
    settle(0, 1)
    forward()
    pass_on(1, 0)
    settle(1, 0)
    backward(0)
    exchange(0).start()
    pass_on(1, 1)
    y_out(0)
    settle(1, 1)
    for n in range(n_c):
        wgrad(1, n)
    backward(1)
    exchange(1).start()
    z_out(1, 0)
    for n in range(n_c):
        wgrad(0, n)
        if n == 0:
            y_out(1)
        if n + 1 < n_c:
            z_out(1, n + 1)
    z_out(0, 0)
    y_in(0)
    for n in range(1, n_c):
        z_out(0, n)
    for n in range(n_c):
        z_in(1, n)
    y_in(1)
    for n in range(n_c):
        z_in(0, n)
    for h in range(2):
        out_own(h).wait()
        out_sib(h).wait()
        exchange(h).wait_send()
        for a in range(2):
            for k in range(1, n_y):
                ag_y(a, h, k).wait_send()
            for k in range(n_y):
                ag_sib(a, h, k).wait_send()
        for k in range(1, n_y):
            ring(h, k).wait_send()
    for kind in range(2):
        for n in range(n_c):
            x_swap(kind, n).wait_send()
            for k in range(1, n_j):
                z_copy(kind, n, k).wait_send()


def hand_over(dx, gin, gout, dx_out, gin_out, gout_out, sem):
    pieces = sem.shape[0] - 2
    band = dx.shape[0] // pieces
    copies = [
        pltpu.make_async_copy(dx.at[pl.ds(i * band, band)], dx_out.at[pl.ds(i * band, band)],
                              sem.at[i])
        for i in range(pieces)
    ]
    copies.append(pltpu.make_async_copy(gin, gin_out, sem.at[pieces]))
    copies.append(pltpu.make_async_copy(gout, gout_out, sem.at[pieces + 1]))
    for copy in copies:
        copy.start()
    for copy in copies:
        copy.wait()


def local(n_dp, n_t, tokens, out_grad, w_in, w_out, block_rows, block_cols):
    tok_count, shard_width = tokens.shape
    cap, side = w_in.shape[0], w_in.shape[1]
    width = shard_width * n_t
    row_count = width // side
    half, wide, span = tok_count // 2, width // 2, side // n_dp
    n_y, n_j = n_t // 2, n_dp // 2
    chunk = 8 if cap % 8 == 0 else cap
    n_q = 2 * (cap // chunk)
    vm, dma = pltpu.VMEM, pltpu.SemaphoreType.DMA
    gathered = vm((n_t, half, shard_width), BF)
    blocks = vm((cap, side, side), BF)
    sums = vm((cap + 1, half, side), F32)
    piece = vm((n_q, n_j, chunk, span, side), BF)
    scratch = [
        pltpu.SMEM((6, max(cap, row_count)), I32),
        gathered, gathered, gathered, gathered,
        vm((row_count, tok_count, side), BF),
        vm((row_count, half, side), BF), vm((row_count, half, side), BF),
        blocks, blocks, vm((cap + 1, tok_count, side), F32), sums, sums,
        vm((cap, tok_count, side), BF), vm((cap, tok_count, side), F32),
        vm((cap, tok_count, side), BF),
        vm((2, 2, half, wide), BF), vm((2, half, wide), BF), vm((2, half, wide), BF),
        vm((2, n_y, half, wide), BF), vm((2, half, wide), BF),
        vm((n_q, 2, n_j, chunk, span, side), BF), piece, piece,
        vm((n_q, max(n_j - 1, 1), chunk, span, side), BF),
        dma((2, 2, n_y - 1)), dma((2, 2, n_y - 1)), dma((2, 2, n_y)), dma((2, 2, n_y)),
        dma((2, 2)), dma((2,)), dma((2,)), dma((2,)), dma((2, n_y - 1)), dma((2, n_y - 1)),
        dma((2,)), dma((2,)), dma((2,)), dma((n_q,)), dma((n_q,)),
        dma((n_q, n_j - 1)), dma((n_q, n_j - 1)),
    ]
    any_space = pl.BlockSpec(memory_space=pl.ANY)
    smem, vmem = pl.BlockSpec(memory_space=pltpu.SMEM), pl.BlockSpec(memory_space=vm)
    shapes = (
        jax.ShapeDtypeStruct((tok_count, width), BF),
        jax.ShapeDtypeStruct((cap, span * side), F32),
        jax.ShapeDtypeStruct((cap, span * side), F32),
    )
    results = pl.pallas_call(
        functools.partial(kernel, n_dp, n_t, chunk),
        out_shape=shapes,
        in_specs=[smem] * 2 + [any_space] * 4,
        out_specs=(any_space, vmem, vmem),
        scratch_shapes=scratch,
        compiler_params=pltpu.CompilerParams(
            collective_id=0, has_side_effects=True, vmem_limit_bytes=56 * 1024 * 1024
        ),
        cost_estimate=pl.CostEstimate(
            flops=10 * cap * tok_count * side * side,
            bytes_accessed=8 * tok_count * width,
            transcendentals=cap * tok_count * side,
        ),
    )(block_rows, block_cols, tokens, out_grad, w_in, w_out)
    return pl.pallas_call(
        hand_over,
        out_shape=shapes,
        in_specs=[any_space] * 3,
        out_specs=(any_space,) * 3,
        scratch_shapes=[dma((10,))],
    )(*results)


def solution(mesh):
    in_specs = (
        P("dp", "tensor"),
        P("dp", "tensor"),
        P("tensor", None, None),
        P("tensor", None, None),
        P("tensor", None),
        P("tensor", None),
    )
    out_specs = (P("dp", None), P("tensor", "dp"), P("tensor", "dp"))
    body = functools.partial(local, mesh.shape["dp"], mesh.shape["tensor"])
    return jax.shard_map(body, mesh=mesh, in_specs=in_specs, out_specs=out_specs, check_vma=False)
```

```python
import functools

import jax
import jax.numpy as jnp
from jax import lax
from jax.experimental import pallas as pl
from jax.experimental.pallas import tpu as pltpu
from jax.sharding import PartitionSpec as P

MESH = pl.DeviceIdType.MESH
BF, F32, I32 = jnp.bfloat16, jnp.float32, jnp.int32
CLIP = 4.0
UNROLL = 4
PREV_COL, END_COL, ROW, LIVE, PREV_ROW, LAST = range(6)


def dot(a, b, ca, cb):
    return lax.dot_general(a, b, (((ca,), (cb,)), ((), ())), preferred_element_type=F32)


def loop(count, body):
    def outer(g, carry):
        for u in range(UNROLL):
            body(g * UNROLL + u)
        return carry

    lax.fori_loop(0, count // UNROLL, outer, 0)


def kernel(
    n_dp, n_t, chunk,
    rows, cols, tok_hbm, grad_hbm, win_hbm, wout_hbm,
    dx_out, gin_out, gout_out,
    table, tok0, tok1, grad0, grad1, tcut, gcut0, gcut1, win, wout, scan_p, scan_h, rscan,
    tok_t, hid_t, gate, dpre, part, rsib, ysum, yrecv, res, stage, xr, zs, zr,
    ag_send, ag_recv, sib_send, sib_recv, loc, wloc, p_send, p_recv, r_send, r_recv,
    o_send, o_recv, o_loc, x_send, x_recv, z_send, z_recv,
):
    cap, side = win.shape[0], win.shape[1]
    half = tok0.shape[1]
    per = tok0.shape[2] // side
    n_y, n_j, n_c = n_t // 2, n_dp // 2, cap // chunk
    row_count = n_t * per
    span = side // n_dp
    wide = row_count * side // 2
    scale = 4194304.0 / n_dp
    d, t = lax.axis_index("dp"), lax.axis_index("tensor")
    c, y = lax.rem(t, 2), t // 2
    sib = y * 2 + (1 - c)
    b, j = lax.rem(d, 2), d // 2
    xpeer = j * 2 + (1 - b)

    def y_at(k):
        return lax.rem(y + k + n_y, n_y) * 2 + c

    def j_at(k):
        return lax.rem(j + k + n_j, n_j)

    barrier = pltpu.get_barrier_semaphore()
    peers = [{"tensor": sib}, {"dp": xpeer}]
    peers += [{"tensor": y_at(k)} for k in range(1, n_y)]
    peers += [{"dp": j_at(k) * 2 + b} for k in range(1, n_j)]
    for peer in peers:
        pl.semaphore_signal(barrier, inc=1, device_id=peer, device_id_type=MESH)

    def remote(src, dst, ss, rs, peer):
        return pltpu.make_async_remote_copy(
            src_ref=src, dst_ref=dst, send_sem=ss, recv_sem=rs, device_id=peer, device_id_type=MESH
        )

    hbm = (tok_hbm, grad_hbm)
    held = ((tok0, tok1), (grad0, grad1))

    def shard(a, h):
        return hbm[a].at[pl.ds(h * half, half), :]

    def ag_y(a, h, k):
        return remote(shard(a, h), held[a][h].at[t], ag_send.at[a, h, k - 1],
                      ag_recv.at[a, h, k - 1], {"tensor": y_at(k)})

    def ag_sib(a, h, k):
        src_t = y_at(-k)
        src = shard(a, h) if k == 0 else held[a][h].at[src_t]
        return remote(src, held[a][h].at[src_t], sib_send.at[a, h, k],
                      sib_recv.at[a, h, k], {"tensor": sib})

    def own(a, h):
        return pltpu.make_async_copy(shard(a, h), held[a][h].at[t], loc.at[a, h])

    weights = [pltpu.make_async_copy(win_hbm, win, wloc.at[0]),
               pltpu.make_async_copy(wout_hbm, wout, wloc.at[1])]

    def start_y(a, h):
        for k in range(1, n_y):
            ag_y(a, h, k).start()

    def pass_on(a, h):
        for k in range(1, n_y):
            ag_y(a, h, k).wait_recv()
            ag_sib(a, h, k).start()

    def settle(a, h):
        own(a, h).wait()
        for k in range(n_y):
            ag_sib(a, h, k).wait_recv()

        def split(g, carry):
            for u in range(per):
                block = held[a][h][g, :, u * side:(u + 1) * side]
                if a == 0:
                    tcut[g * per + u, h * half:(h + 1) * half, :] = block
                else:
                    (gcut0, gcut1)[h][g * per + u] = block
            return carry

        lax.fori_loop(0, n_t, split, 0)

    def tables():
        def of_slot(s, carry):
            col, row = cols[0, s], rows[0, s]
            prev_col, prev_row, end_col = I32(cap), I32(cap), I32(0)
            for q in range(cap):
                same_col, same_row = cols[0, q] == col, rows[0, q] == row
                prev_col = jnp.where(same_col & (q < s), q, prev_col)
                prev_row = jnp.where(same_row & (q < s), q, prev_row)
                end_col = jnp.where(same_col, q, end_col)
            table[PREV_COL, s] = prev_col
            table[PREV_ROW, s] = prev_row
            table[END_COL, s] = end_col
            table[ROW, s] = jnp.maximum(row, 0)
            table[LIVE, s] = jnp.where(row >= 0, 1, 0)
            return carry

        def of_row(r, carry):
            last = I32(cap)
            for q in range(cap):
                last = jnp.where(rows[0, q] == r, q, last)
            table[LAST, r] = last
            return carry

        lax.fori_loop(0, cap, of_slot, 0)
        lax.fori_loop(0, row_count, of_row, 0)

    def forward():
        def body(s):
            block = tcut[table[ROW, s]]
            tok_t[s] = block.T
            term = dot(block, win[s], 1, 0)
            scan_p[s] = term + scan_p[table[PREV_COL, s]]

        loop(cap, body)

        def point(s):
            pre = scan_p[table[END_COL, s]]
            sigma = 1.0 / (1.0 + jnp.exp(-pre))
            hid_t[s] = (pre * sigma).astype(BF).T
            gate[s] = sigma * (1.0 + pre * (1.0 - sigma))

        loop(cap, point)

    def backward(h, between=None):
        at = pl.ds(h * half, half)

        def body(s):
            term = dot((gcut0, gcut1)[h][table[ROW, s]], wout[s], 1, 1)
            scan_h[s] = term + scan_h[table[PREV_COL, s]]

        loop(cap, body)

        def point(s):
            dpre[s, at, :] = (scan_h[table[END_COL, s]] * gate[s, at, :]).astype(BF)

        loop(cap, point)

        if between is not None:
            between()

        def term(s):
            rscan[s] = dot(dpre[s, at, :], win[s], 1, 1) + rscan[table[PREV_ROW, s]]

        loop(cap, term)
        for r in range(row_count):
            at_half, off = divmod(r * side, wide)
            part[h, at_half, :, pl.ds(off, side)] = rscan[table[LAST, r]].astype(BF)

    def exchange(h):
        return remote(part.at[h, 1 - c], rsib.at[h], p_send.at[h], p_recv.at[h], {"tensor": sib})

    def ring(h, k):
        return remote(ysum.at[h], yrecv.at[h, y], r_send.at[h, k - 1], r_recv.at[h, k - 1],
                      {"tensor": y_at(k)})

    def y_out(h):
        exchange(h).wait_recv()

        def band(i, carry):
            at = pl.ds(pl.multiple_of(i * 16, 16), 16)
            ysum[h, at, :] = (
                part[h, c, at, :].astype(F32) + rsib[h, at, :].astype(F32)
            ).astype(BF)
            return carry

        lax.fori_loop(0, half // 16, band, 0)
        for k in range(1, n_y):
            ring(h, k).start()

    def out_at(h):
        return dx_out.at[pl.ds(h * half, half), pl.ds(pl.multiple_of(c * wide, side), wide)]

    def out_sib(h):
        return remote(res.at[h], out_at(h), o_send.at[h], o_recv.at[h], {"tensor": sib})

    def out_own(h):
        return pltpu.make_async_copy(res.at[h], out_at(h), o_loc.at[h])

    def y_in(h):
        for k in range(1, n_y):
            ring(h, k).wait_recv()

        def band(i, carry):
            at = pl.ds(pl.multiple_of(i * 16, 16), 16)
            mine = ysum[h, at, :].astype(F32)
            acc = jnp.zeros_like(mine)
            for g in range(n_y):
                acc = acc + jnp.where(y == g, mine, yrecv[h, g, at, :].astype(F32))
            res[h, at, :] = acc.astype(BF)
            return carry

        lax.fori_loop(0, half // 16, band, 0)
        out_sib(h).start()
        out_own(h).start()

    g_out = (gin_out, gout_out)

    def x_swap(kind, n):
        q = kind * n_c + n
        return remote(stage.at[q, 1 - b], xr.at[q], x_send.at[q], x_recv.at[q], {"dp": xpeer})

    def wgrad(kind, n):
        def body(i):
            s = n * chunk + i
            if kind == 0:
                g = dot(tok_t[s], dpre[s], 1, 0)
            else:
                row = table[ROW, s]
                g = dot(hid_t[s], jnp.concatenate([gcut0[row], gcut1[row]], 0), 1, 0)
            bins = jnp.floor(jnp.clip(g, -CLIP, CLIP) * scale) * table[LIVE, s].astype(F32)
            bins = bins.astype(BF)
            for p in range(n_dp):
                stage[kind * n_c + n, p % 2, p // 2, i] = bins[p * span:(p + 1) * span]

        loop(chunk, body)
        x_swap(kind, n).start()

    def z_copy(kind, n, k):
        q = kind * n_c + n
        return remote(zs.at[q, j_at(k)], zr.at[q, k - 1], z_send.at[q, k - 1],
                      z_recv.at[q, k - 1], {"dp": j_at(k) * 2 + b})

    def z_out(kind, n):
        q = kind * n_c + n
        x_swap(kind, n).wait_recv()
        for k in list(range(1, n_j)) + [0]:
            g = j_at(k)
            zs[q, g] = (stage[q, b, g].astype(F32) + xr[q, g].astype(F32)).astype(BF)
            if k:
                z_copy(kind, n, k).start()

    def z_in(kind, n):
        q = kind * n_c + n
        acc = zs[q, j].astype(F32)
        for k in range(1, n_j):
            z_copy(kind, n, k).wait_recv()
            acc = acc + zr[q, k - 1].astype(F32)
        acc = acc * (1.0 / scale)
        for r in range(span):
            g_out[kind][n * chunk:(n + 1) * chunk, r * side:(r + 1) * side] = acc[:, r, :]

    for w in weights:
        w.start()
    for a in range(2):
        for h in range(2):
            own(a, h).start()
    pl.semaphore_wait(barrier, len(peers))
    start_y(0, 0)
    start_y(0, 1)
    for a in range(2):
        for h in range(2):
            ag_sib(a, h, 0).start()
    tables()
    scan_p[cap] = jnp.zeros(scan_p.shape[1:], F32)
    scan_h[cap] = jnp.zeros(scan_h.shape[1:], F32)
    rscan[cap] = jnp.zeros(rscan.shape[1:], F32)
    pass_on(0, 0)
    start_y(1, 0)
    pass_on(0, 1)
    start_y(1, 1)
    for w in weights:
        w.wait()
    settle(0, 0)
    settle(0, 1)
    forward()
    pass_on(1, 0)
    settle(1, 0)
    backward(0)
    exchange(0).start()
    pass_on(1, 1)
    y_out(0)
    settle(1, 1)
    for n in range(n_c):
        wgrad(1, n)
    backward(1, lambda: z_out(1, 0))
    exchange(1).start()
    for n in range(n_c):
        wgrad(0, n)
        if n == 0:
            y_out(1)
        if n + 1 < n_c:
            z_out(1, n + 1)
    z_out(0, 0)
    y_in(0)
    for n in range(1, n_c):
        z_out(0, n)
    for n in range(n_c):
        z_in(1, n)
    y_in(1)
    for n in range(n_c):
        z_in(0, n)
    for h in range(2):
        out_own(h).wait()
        out_sib(h).wait()
        exchange(h).wait_send()
        for a in range(2):
            for k in range(1, n_y):
                ag_y(a, h, k).wait_send()
            for k in range(n_y):
                ag_sib(a, h, k).wait_send()
        for k in range(1, n_y):
            ring(h, k).wait_send()
    for kind in range(2):
        for n in range(n_c):
            x_swap(kind, n).wait_send()
            for k in range(1, n_j):
                z_copy(kind, n, k).wait_send()


def hand_over(dx, gin, gout, dx_out, gin_out, gout_out, dx_held, gin_held, gout_held, sem_in, sem_out):
    pieces = sem_in.shape[0] - 2
    band = dx.shape[0] // pieces
    at = [pl.ds(i * band, band) for i in range(pieces)]
    legs = [(dx.at[w], dx_held.at[w], dx_out.at[w]) for w in at]
    legs += [(gin, gin_held, gin_out), (gout, gout_held, gout_out)]
    arrive = [pltpu.make_async_copy(a, h, sem_in.at[i]) for i, (a, h, _) in enumerate(legs)]
    leave = [pltpu.make_async_copy(h, o, sem_out.at[i]) for i, (_, h, o) in enumerate(legs)]
    for copy in arrive:
        copy.start()
    for first, second in zip(arrive, leave):
        first.wait()
        second.start()
    for copy in leave:
        copy.wait()


def local(n_dp, n_t, tokens, out_grad, w_in, w_out, block_rows, block_cols):
    tok_count, shard_width = tokens.shape
    cap, side = w_in.shape[0], w_in.shape[1]
    width = shard_width * n_t
    row_count = width // side
    half, wide, span = tok_count // 2, width // 2, side // n_dp
    n_y, n_j = n_t // 2, n_dp // 2
    chunk = 8 if cap % 8 == 0 else cap
    n_q = 2 * (cap // chunk)
    vm, dma = pltpu.VMEM, pltpu.SemaphoreType.DMA
    gathered = vm((n_t, half, shard_width), BF)
    blocks = vm((cap, side, side), BF)
    sums = vm((cap + 1, half, side), F32)
    piece = vm((n_q, n_j, chunk, span, side), BF)
    scratch = [
        pltpu.SMEM((6, max(cap, row_count)), I32),
        gathered, gathered, gathered, gathered,
        vm((row_count, tok_count, side), BF),
        vm((row_count, half, side), BF), vm((row_count, half, side), BF),
        blocks, blocks, vm((cap + 1, tok_count, side), F32), sums, sums,
        vm((cap, side, tok_count), BF), vm((cap, side, tok_count), BF),
        vm((cap, tok_count, side), F32),
        vm((cap, tok_count, side), BF),
        vm((2, 2, half, wide), BF), vm((2, half, wide), BF), vm((2, half, wide), BF),
        vm((2, n_y, half, wide), BF), vm((2, half, wide), BF),
        vm((n_q, 2, n_j, chunk, span, side), BF), piece, piece,
        vm((n_q, max(n_j - 1, 1), chunk, span, side), BF),
        dma((2, 2, n_y - 1)), dma((2, 2, n_y - 1)), dma((2, 2, n_y)), dma((2, 2, n_y)),
        dma((2, 2)), dma((2,)), dma((2,)), dma((2,)), dma((2, n_y - 1)), dma((2, n_y - 1)),
        dma((2,)), dma((2,)), dma((2,)), dma((n_q,)), dma((n_q,)),
        dma((n_q, n_j - 1)), dma((n_q, n_j - 1)),
    ]
    any_space = pl.BlockSpec(memory_space=pl.ANY)
    smem, vmem = pl.BlockSpec(memory_space=pltpu.SMEM), pl.BlockSpec(memory_space=vm)
    shapes = (
        jax.ShapeDtypeStruct((tok_count, width), BF),
        jax.ShapeDtypeStruct((cap, span * side), F32),
        jax.ShapeDtypeStruct((cap, span * side), F32),
    )
    results = pl.pallas_call(
        functools.partial(kernel, n_dp, n_t, chunk),
        out_shape=shapes,
        in_specs=[smem] * 2 + [any_space] * 4,
        out_specs=(any_space, vmem, vmem),
        scratch_shapes=scratch,
        compiler_params=pltpu.CompilerParams(
            collective_id=0, has_side_effects=True, vmem_limit_bytes=56 * 1024 * 1024
        ),
        cost_estimate=pl.CostEstimate(
            flops=10 * cap * tok_count * side * side,
            bytes_accessed=8 * tok_count * width,
            transcendentals=cap * tok_count * side,
        ),
    )(block_rows, block_cols, tokens, out_grad, w_in, w_out)
    return pl.pallas_call(
        hand_over,
        out_shape=shapes,
        in_specs=[any_space] * 3,
        out_specs=(any_space,) * 3,
        scratch_shapes=[vm(v.shape, v.dtype) for v in shapes] + [dma((10,)), dma((10,))],
        compiler_params=pltpu.CompilerParams(vmem_limit_bytes=56 * 1024 * 1024),
    )(*results)


def solution(mesh):
    in_specs = (
        P("dp", "tensor"),
        P("dp", "tensor"),
        P("tensor", None, None),
        P("tensor", None, None),
        P("tensor", None),
        P("tensor", None),
    )
    out_specs = (P("dp", None), P("tensor", "dp"), P("tensor", "dp"))
    body = functools.partial(local, mesh.shape["dp"], mesh.shape["tensor"])
    return jax.shard_map(body, mesh=mesh, in_specs=in_specs, out_specs=out_specs, check_vma=False)
```

```python
import functools

import jax
import jax.numpy as jnp
from jax import lax
from jax.experimental import pallas as pl
from jax.experimental.pallas import tpu as pltpu
from jax.sharding import PartitionSpec as P

MESH = pl.DeviceIdType.MESH
BF, F32, I32 = jnp.bfloat16, jnp.float32, jnp.int32
CLIP = 4.0
UNROLL = 4
PREV_COL, END_COL, ROW, LIVE, PREV_ROW, LAST = range(6)


def dot(a, b, ca, cb):
    return lax.dot_general(a, b, (((ca,), (cb,)), ((), ())), preferred_element_type=F32)


def loop(count, body):
    def outer(g, carry):
        for u in range(UNROLL):
            body(g * UNROLL + u)
        return carry

    lax.fori_loop(0, count // UNROLL, outer, 0)


def loop_pairs(count, make, use):
    def outer(g, carry):
        at = [g * UNROLL + u for u in range(UNROLL)]
        made = [make(i) for i in at]
        for i, value in zip(at, made):
            use(i, value)
        return carry

    lax.fori_loop(0, count // UNROLL, outer, 0)


def kernel(
    n_dp, n_t, chunk,
    rows, cols, tok_hbm, grad_hbm, win_hbm, wout_hbm,
    dx_out, gin_out, gout_out,
    table, tok0, tok1, grad0, grad1, tcut0, tcut1, gcut0, gcut1, win, wout, scan, rscan,
    tok_t, hid_t, gate, dpre, part, rsib, ysum, yrecv, res, stage, xr, zs, zr,
    ag_send, ag_recv, sib_send, sib_recv, loc, wloc, p_send, p_recv, r_send, r_recv,
    o_send, o_recv, o_loc, x_send, x_recv, z_send, z_recv,
):
    cap, side = win.shape[0], win.shape[1]
    half = tok0.shape[1]
    per = tok0.shape[2] // side
    n_y, n_j, n_c = n_t // 2, n_dp // 2, cap // chunk
    row_count = n_t * per
    span = side // n_dp
    wide = row_count * side // 2
    scale = 4194304.0 / n_dp
    d, t = lax.axis_index("dp"), lax.axis_index("tensor")
    c, y = lax.rem(t, 2), t // 2
    sib = y * 2 + (1 - c)
    b, j = lax.rem(d, 2), d // 2
    xpeer = j * 2 + (1 - b)

    def y_at(k):
        return lax.rem(y + k + n_y, n_y) * 2 + c

    def j_at(k):
        return lax.rem(j + k + n_j, n_j)

    barrier = pltpu.get_barrier_semaphore()
    peers = [{"tensor": sib}, {"dp": xpeer}]
    peers += [{"tensor": y_at(k)} for k in range(1, n_y)]
    peers += [{"dp": j_at(k) * 2 + b} for k in range(1, n_j)]
    for peer in peers:
        pl.semaphore_signal(barrier, inc=1, device_id=peer, device_id_type=MESH)

    def remote(src, dst, ss, rs, peer):
        return pltpu.make_async_remote_copy(
            src_ref=src, dst_ref=dst, send_sem=ss, recv_sem=rs, device_id=peer, device_id_type=MESH
        )

    hbm = (tok_hbm, grad_hbm)
    held = ((tok0, tok1), (grad0, grad1))
    cut = ((tcut0, tcut1), (gcut0, gcut1))

    def shard(a, h):
        return hbm[a].at[pl.ds(h * half, half), :]

    def ag_y(a, h, k):
        return remote(shard(a, h), held[a][h].at[t], ag_send.at[a, h, k - 1],
                      ag_recv.at[a, h, k - 1], {"tensor": y_at(k)})

    def ag_sib(a, h, k):
        src_t = y_at(-k)
        src = shard(a, h) if k == 0 else held[a][h].at[src_t]
        return remote(src, held[a][h].at[src_t], sib_send.at[a, h, k],
                      sib_recv.at[a, h, k], {"tensor": sib})

    def own(a, h):
        return pltpu.make_async_copy(shard(a, h), held[a][h].at[t], loc.at[a, h])

    weights = [pltpu.make_async_copy(win_hbm, win, wloc.at[0]),
               pltpu.make_async_copy(wout_hbm, wout, wloc.at[1])]

    def start_y(a, h):
        for k in range(1, n_y):
            ag_y(a, h, k).start()

    def pass_on(a, h):
        for k in range(1, n_y):
            ag_y(a, h, k).wait_recv()
            ag_sib(a, h, k).start()

    def settle(a, h):
        own(a, h).wait()
        for k in range(n_y):
            ag_sib(a, h, k).wait_recv()

        def split(g, carry):
            for u in range(per):
                cut[a][h][g * per + u] = held[a][h][g, :, u * side:(u + 1) * side]
            return carry

        lax.fori_loop(0, n_t, split, 0)

    def tables():
        for s in range(cap):
            col, row = cols[0, s], rows[0, s]
            prev_col, prev_row, end_col = I32(cap), I32(cap), I32(s)
            for q in range(s):
                prev_col = jnp.where(cols[0, q] == col, q, prev_col)
                prev_row = jnp.where(rows[0, q] == row, q, prev_row)
            for q in range(s + 1, cap):
                end_col = jnp.where(cols[0, q] == col, q, end_col)
            table[PREV_COL, s] = prev_col
            table[PREV_ROW, s] = prev_row
            table[END_COL, s] = end_col
            table[ROW, s] = jnp.maximum(row, 0)
            table[LIVE, s] = jnp.where(row >= 0, 1, 0)

        def of_row(r, carry):
            last = I32(cap)
            for q in range(cap):
                last = jnp.where(rows[0, q] == r, q, last)
            table[LAST, r] = last
            return carry

        lax.fori_loop(0, row_count, of_row, 0)

    def forward(h):
        at = slice(h * half, (h + 1) * half)

        def make(s):
            block = cut[0][h][table[ROW, s]]
            return block.T, dot(block, win[s], 1, 0)

        def use(s, made):
            tok_t[s, :, at] = made[0]
            scan[s] = made[1] + scan[table[PREV_COL, s]]

        loop_pairs(cap, make, use)

        def point(s):
            pre = scan[table[END_COL, s]]
            sigma = 1.0 / (1.0 + jnp.exp(-pre))
            hid_t[s, :, at] = (pre * sigma).astype(BF).T
            gate[s, at, :] = sigma * (1.0 + pre * (1.0 - sigma))

        loop(cap, point)

    def backward(h, between=None):
        at = pl.ds(h * half, half)

        def make(s):
            return dot(cut[1][h][table[ROW, s]], wout[s], 1, 1)

        def use(s, made):
            scan[s] = made + scan[table[PREV_COL, s]]

        loop_pairs(cap, make, use)

        def point(s):
            dpre[s, at, :] = (scan[table[END_COL, s]] * gate[s, at, :]).astype(BF)

        loop(cap, point)
        if between is not None:
            between()

        def make_term(s):
            return dot(dpre[s, at, :], win[s], 1, 1)

        def use_term(s, made):
            rscan[s] = made + rscan[table[PREV_ROW, s]]

        loop_pairs(cap, make_term, use_term)
        for r in range(row_count):
            at_half, off = divmod(r * side, wide)
            part[h, at_half, :, pl.ds(off, side)] = rscan[table[LAST, r]].astype(BF)

    def exchange(h):
        return remote(part.at[h, 1 - c], rsib.at[h], p_send.at[h], p_recv.at[h], {"tensor": sib})

    def ring(h, k):
        return remote(ysum.at[h], yrecv.at[h, y], r_send.at[h, k - 1], r_recv.at[h, k - 1],
                      {"tensor": y_at(k)})

    def y_out(h):
        exchange(h).wait_recv()

        def band(i, carry):
            at = pl.ds(pl.multiple_of(i * 16, 16), 16)
            ysum[h, at, :] = (
                part[h, c, at, :].astype(F32) + rsib[h, at, :].astype(F32)
            ).astype(BF)
            return carry

        lax.fori_loop(0, half // 16, band, 0)
        for k in range(1, n_y):
            ring(h, k).start()

    def out_at(h):
        return dx_out.at[pl.ds(h * half, half), pl.ds(pl.multiple_of(c * wide, side), wide)]

    def out_sib(h):
        return remote(res.at[h], out_at(h), o_send.at[h], o_recv.at[h], {"tensor": sib})

    def out_own(h):
        return pltpu.make_async_copy(res.at[h], out_at(h), o_loc.at[h])

    def y_in(h):
        for k in range(1, n_y):
            ring(h, k).wait_recv()

        def band(i, carry):
            at = pl.ds(pl.multiple_of(i * 16, 16), 16)
            mine = ysum[h, at, :].astype(F32)
            acc = jnp.zeros_like(mine)
            for g in range(n_y):
                acc = acc + jnp.where(y == g, mine, yrecv[h, g, at, :].astype(F32))
            res[h, at, :] = acc.astype(BF)
            return carry

        lax.fori_loop(0, half // 16, band, 0)
        out_sib(h).start()
        out_own(h).start()

    g_out = (gin_out, gout_out)

    def x_swap(kind, n):
        q = kind * n_c + n
        return remote(stage.at[q, 1 - b], xr.at[q], x_send.at[q], x_recv.at[q], {"dp": xpeer})

    def wgrad(kind, n):
        def make(i):
            s = n * chunk + i
            if kind == 0:
                return dot(tok_t[s], dpre[s], 1, 0)
            row = table[ROW, s]
            return dot(hid_t[s], jnp.concatenate([gcut0[row], gcut1[row]], 0), 1, 0)

        def use(i, g):
            live = table[LIVE, n * chunk + i].astype(F32)
            bins = (jnp.floor(jnp.clip(g, -CLIP, CLIP) * scale) * live).astype(BF)
            for p in range(n_dp):
                stage[kind * n_c + n, p % 2, p // 2, i] = bins[p * span:(p + 1) * span]

        loop_pairs(chunk, make, use)
        x_swap(kind, n).start()

    def z_copy(kind, n, k):
        q = kind * n_c + n
        return remote(zs.at[q, j_at(k)], zr.at[q, k - 1], z_send.at[q, k - 1],
                      z_recv.at[q, k - 1], {"dp": j_at(k) * 2 + b})

    def z_out(kind, n):
        q = kind * n_c + n
        x_swap(kind, n).wait_recv()
        for k in list(range(1, n_j)) + [0]:
            g = j_at(k)
            zs[q, g] = (stage[q, b, g].astype(F32) + xr[q, g].astype(F32)).astype(BF)
            if k:
                z_copy(kind, n, k).start()

    def z_in(kind, n):
        q = kind * n_c + n
        acc = zs[q, j].astype(F32)
        for k in range(1, n_j):
            z_copy(kind, n, k).wait_recv()
            acc = acc + zr[q, k - 1].astype(F32)
        acc = acc * (1.0 / scale)
        for r in range(span):
            g_out[kind][n * chunk:(n + 1) * chunk, r * side:(r + 1) * side] = acc[:, r, :]

    for w in weights:
        w.start()
    for a in range(2):
        for h in range(2):
            own(a, h).start()
    pl.semaphore_wait(barrier, len(peers))
    start_y(0, 0)
    for a in range(2):
        for h in range(2):
            ag_sib(a, h, 0).start()
    tables()
    start_y(0, 1)
    scan[cap] = jnp.zeros(scan.shape[1:], F32)
    rscan[cap] = jnp.zeros(rscan.shape[1:], F32)
    pass_on(0, 0)
    start_y(1, 0)
    for w in weights:
        w.wait()
    settle(0, 0)
    forward(0)
    pass_on(0, 1)
    start_y(1, 1)
    settle(0, 1)
    forward(1)
    pass_on(1, 0)
    settle(1, 0)
    backward(0)
    exchange(0).start()
    y_out(0)
    pass_on(1, 1)
    settle(1, 1)
    for n in range(n_c):
        wgrad(1, n)
    backward(1, lambda: z_out(1, 0))
    exchange(1).start()
    for n in range(n_c):
        wgrad(0, n)
        if n == 0:
            y_out(1)
        if n + 1 < n_c:
            z_out(1, n + 1)
    z_out(0, 0)
    y_in(0)
    for n in range(1, n_c):
        z_out(0, n)
    for n in range(n_c):
        z_in(1, n)
    y_in(1)
    for n in range(n_c):
        z_in(0, n)
    for h in range(2):
        out_own(h).wait()
        out_sib(h).wait()
        exchange(h).wait_send()
        for a in range(2):
            for k in range(1, n_y):
                ag_y(a, h, k).wait_send()
            for k in range(n_y):
                ag_sib(a, h, k).wait_send()
        for k in range(1, n_y):
            ring(h, k).wait_send()
    for kind in range(2):
        for n in range(n_c):
            x_swap(kind, n).wait_send()
            for k in range(1, n_j):
                z_copy(kind, n, k).wait_send()


def hand_over(dx, gin, gout, dx_out, gin_out, gout_out, dx_held, gin_held, gout_held, sem_in, sem_out):
    pieces = sem_in.shape[0] - 2
    band = dx.shape[0] // pieces
    at = [pl.ds(i * band, band) for i in range(pieces)]
    legs = [(dx.at[w], dx_held.at[w], dx_out.at[w]) for w in at]
    legs += [(gin, gin_held, gin_out), (gout, gout_held, gout_out)]
    arrive = [pltpu.make_async_copy(a, h, sem_in.at[i]) for i, (a, h, _) in enumerate(legs)]
    leave = [pltpu.make_async_copy(h, o, sem_out.at[i]) for i, (_, h, o) in enumerate(legs)]
    for copy in arrive:
        copy.start()
    for first, second in zip(arrive, leave):
        first.wait()
        second.start()
    for copy in leave:
        copy.wait()


def local(n_dp, n_t, tokens, out_grad, w_in, w_out, block_rows, block_cols):
    tok_count, shard_width = tokens.shape
    cap, side = w_in.shape[0], w_in.shape[1]
    width = shard_width * n_t
    row_count = width // side
    half, wide, span = tok_count // 2, width // 2, side // n_dp
    n_y, n_j = n_t // 2, n_dp // 2
    chunk = 8 if cap % 8 == 0 else cap
    n_q = 2 * (cap // chunk)
    vm, dma = pltpu.VMEM, pltpu.SemaphoreType.DMA
    gathered = vm((n_t, half, shard_width), BF)
    cuts = vm((row_count, half, side), BF)
    blocks = vm((cap, side, side), BF)
    sums = vm((cap + 1, half, side), F32)
    piece = vm((n_q, n_j, chunk, span, side), BF)
    scratch = [
        pltpu.SMEM((6, max(cap, row_count)), I32),
        gathered, gathered, gathered, gathered,
        cuts, cuts, cuts, cuts, blocks, blocks, sums, sums,
        vm((cap, side, tok_count), BF), vm((cap, side, tok_count), BF),
        vm((cap, tok_count, side), F32),
        vm((cap, tok_count, side), BF),
        vm((2, 2, half, wide), BF), vm((2, half, wide), BF), vm((2, half, wide), BF),
        vm((2, n_y, half, wide), BF), vm((2, half, wide), BF),
        vm((n_q, 2, n_j, chunk, span, side), BF), piece, piece,
        vm((n_q, max(n_j - 1, 1), chunk, span, side), BF),
        dma((2, 2, n_y - 1)), dma((2, 2, n_y - 1)), dma((2, 2, n_y)), dma((2, 2, n_y)),
        dma((2, 2)), dma((2,)), dma((2,)), dma((2,)), dma((2, n_y - 1)), dma((2, n_y - 1)),
        dma((2,)), dma((2,)), dma((2,)), dma((n_q,)), dma((n_q,)),
        dma((n_q, n_j - 1)), dma((n_q, n_j - 1)),
    ]
    any_space = pl.BlockSpec(memory_space=pl.ANY)
    smem, vmem = pl.BlockSpec(memory_space=pltpu.SMEM), pl.BlockSpec(memory_space=vm)
    shapes = (
        jax.ShapeDtypeStruct((tok_count, width), BF),
        jax.ShapeDtypeStruct((cap, span * side), F32),
        jax.ShapeDtypeStruct((cap, span * side), F32),
    )
    results = pl.pallas_call(
        functools.partial(kernel, n_dp, n_t, chunk),
        out_shape=shapes,
        in_specs=[smem] * 2 + [any_space] * 4,
        out_specs=(any_space, vmem, vmem),
        scratch_shapes=scratch,
        compiler_params=pltpu.CompilerParams(
            collective_id=0, has_side_effects=True, vmem_limit_bytes=56 * 1024 * 1024
        ),
        cost_estimate=pl.CostEstimate(
            flops=10 * cap * tok_count * side * side,
            bytes_accessed=8 * tok_count * width,
            transcendentals=cap * tok_count * side,
        ),
    )(block_rows, block_cols, tokens, out_grad, w_in, w_out)
    return pl.pallas_call(
        hand_over,
        out_shape=shapes,
        in_specs=[any_space] * 3,
        out_specs=(any_space,) * 3,
        scratch_shapes=[vm(v.shape, v.dtype) for v in shapes] + [dma((10,)), dma((10,))],
        compiler_params=pltpu.CompilerParams(vmem_limit_bytes=56 * 1024 * 1024),
    )(*results)


def solution(mesh):
    in_specs = (
        P("dp", "tensor"),
        P("dp", "tensor"),
        P("tensor", None, None),
        P("tensor", None, None),
        P("tensor", None),
        P("tensor", None),
    )
    out_specs = (P("dp", None), P("tensor", "dp"), P("tensor", "dp"))
    body = functools.partial(local, mesh.shape["dp"], mesh.shape["tensor"])
    return jax.shard_map(body, mesh=mesh, in_specs=in_specs, out_specs=out_specs, check_vma=False)
```

```python
import functools

import jax
import jax.numpy as jnp
from jax import lax
from jax.experimental import pallas as pl
from jax.experimental.pallas import tpu as pltpu
from jax.sharding import PartitionSpec as P

MESH = pl.DeviceIdType.MESH
BF, F32, I32 = jnp.bfloat16, jnp.float32, jnp.int32
CLIP = 4.0
UNROLL = 4
PREV_COL, END_COL, ROW, LIVE, PREV_ROW, LAST = range(6)


def dot(a, b, ca, cb):
    return lax.dot_general(a, b, (((ca,), (cb,)), ((), ())), preferred_element_type=F32)


def loop(count, body):
    def outer(g, carry):
        for u in range(UNROLL):
            body(g * UNROLL + u)
        return carry

    lax.fori_loop(0, count // UNROLL, outer, 0)


def loop_pairs(count, make, use):
    def outer(g, carry):
        at = [g * UNROLL + u for u in range(UNROLL)]
        made = [make(i) for i in at]
        for i, value in zip(at, made):
            use(i, value)
        return carry

    lax.fori_loop(0, count // UNROLL, outer, 0)


def kernel(
    n_dp, n_t, chunk,
    rows, cols, tok_hbm, grad_hbm, win_hbm, wout_hbm,
    dx_out, gin_out, gout_out,
    table, tok0, tok1, grad0, grad1, tcut0, tcut1, gcut0, gcut1, win, wout, scan, rscan,
    tok_t, hid_t, gate, dpre, part, rsib, ysum, yrecv, res, stage, xr, zs, zr,
    ag_send, ag_recv, sib_send, sib_recv, loc, wloc, p_send, p_recv, r_send, r_recv,
    o_send, o_recv, o_loc, x_send, x_recv, z_send, z_recv,
):
    cap, side = win.shape[0], win.shape[1]
    half = tok0.shape[1]
    per = tok0.shape[2] // side
    n_y, n_j, n_c = n_t // 2, n_dp // 2, cap // chunk
    row_count = n_t * per
    span = side // n_dp
    wide = row_count * side // 2
    scale = 4194304.0 / n_dp
    d, t = lax.axis_index("dp"), lax.axis_index("tensor")
    c, y = lax.rem(t, 2), t // 2
    sib = y * 2 + (1 - c)
    b, j = lax.rem(d, 2), d // 2
    xpeer = j * 2 + (1 - b)

    def y_at(k):
        return lax.rem(y + k + n_y, n_y) * 2 + c

    def j_at(k):
        return lax.rem(j + k + n_j, n_j)

    barrier = pltpu.get_barrier_semaphore()
    peers = [{"tensor": sib}, {"dp": xpeer}]
    peers += [{"tensor": y_at(k)} for k in range(1, n_y)]
    peers += [{"dp": j_at(k) * 2 + b} for k in range(1, n_j)]
    for peer in peers:
        pl.semaphore_signal(barrier, inc=1, device_id=peer, device_id_type=MESH)

    def remote(src, dst, ss, rs, peer):
        return pltpu.make_async_remote_copy(
            src_ref=src, dst_ref=dst, send_sem=ss, recv_sem=rs, device_id=peer, device_id_type=MESH
        )

    hbm = (tok_hbm, grad_hbm)
    held = ((tok0, tok1), (grad0, grad1))
    cut = ((tcut0, tcut1), (gcut0, gcut1))

    def shard(a, h):
        return hbm[a].at[pl.ds(h * half, half), :]

    def ag_y(a, h, k):
        return remote(shard(a, h), held[a][h].at[t], ag_send.at[a, h, k - 1],
                      ag_recv.at[a, h, k - 1], {"tensor": y_at(k)})

    def ag_sib(a, h, k):
        src_t = y_at(-k)
        src = shard(a, h) if k == 0 else held[a][h].at[src_t]
        return remote(src, held[a][h].at[src_t], sib_send.at[a, h, k],
                      sib_recv.at[a, h, k], {"tensor": sib})

    def own(a, h):
        return pltpu.make_async_copy(shard(a, h), held[a][h].at[t], loc.at[a, h])

    weights = [pltpu.make_async_copy(win_hbm, win, wloc.at[0]),
               pltpu.make_async_copy(wout_hbm, wout, wloc.at[1])]

    def start_y(a, h):
        for k in range(1, n_y):
            ag_y(a, h, k).start()

    def pass_on(a, h):
        for k in range(1, n_y):
            ag_y(a, h, k).wait_recv()
            ag_sib(a, h, k).start()

    def settle(a, h):
        own(a, h).wait()
        for k in range(n_y):
            ag_sib(a, h, k).wait_recv()

        def split(g, carry):
            for u in range(per):
                cut[a][h][g * per + u] = held[a][h][g, :, u * side:(u + 1) * side]
            return carry

        lax.fori_loop(0, n_t, split, 0)

    def tables():
        for s in range(cap):
            col, row = cols[0, s], rows[0, s]
            prev_col, prev_row, end_col = I32(cap), I32(cap), I32(s)
            for q in range(s):
                prev_col = jnp.where(cols[0, q] == col, q, prev_col)
                prev_row = jnp.where(rows[0, q] == row, q, prev_row)
            for q in range(s + 1, cap):
                end_col = jnp.where(cols[0, q] == col, q, end_col)
            table[PREV_COL, s] = prev_col
            table[PREV_ROW, s] = prev_row
            table[END_COL, s] = end_col
            table[ROW, s] = jnp.maximum(row, 0)
            table[LIVE, s] = jnp.where(row >= 0, 1, 0)

        def of_row(r, carry):
            last = I32(cap)
            for q in range(cap):
                last = jnp.where(rows[0, q] == r, q, last)
            table[LAST, r] = last
            return carry

        lax.fori_loop(0, row_count, of_row, 0)

    def forward(h):
        at = slice(h * half, (h + 1) * half)

        def make(s):
            block = cut[0][h][table[ROW, s]]
            return block.T, dot(block, win[s], 1, 0)

        def use(s, made):
            tok_t[s, :, at] = made[0]
            scan[s] = made[1] + scan[table[PREV_COL, s]]

        loop_pairs(cap, make, use)

        def point(s):
            pre = scan[table[END_COL, s]]
            sigma = 1.0 / (1.0 + jnp.exp(-pre))
            hid_t[s, :, at] = (pre * sigma).astype(BF).T
            gate[s, at, :] = sigma * (1.0 + pre * (1.0 - sigma))

        loop(cap, point)

    def backward(h, between=None):
        at = pl.ds(h * half, half)

        def make(s):
            return dot(cut[1][h][table[ROW, s]], wout[s], 1, 1)

        def use(s, made):
            scan[s] = made + scan[table[PREV_COL, s]]

        loop_pairs(cap, make, use)

        def point(s):
            dpre[s, at, :] = (scan[table[END_COL, s]] * gate[s, at, :]).astype(BF)

        loop(cap, point)
        if between is not None:
            between()

        def make_term(s):
            return dot(dpre[s, at, :], win[s], 1, 1)

        def use_term(s, made):
            rscan[s] = made + rscan[table[PREV_ROW, s]]

        loop_pairs(cap, make_term, use_term)
        for r in range(row_count):
            at_half, off = divmod(r * side, wide)
            part[h, at_half, :, pl.ds(off, side)] = rscan[table[LAST, r]].astype(BF)

    def exchange(h):
        return remote(part.at[h, 1 - c], rsib.at[h], p_send.at[h], p_recv.at[h], {"tensor": sib})

    parts = 2
    piece = half // parts

    def ring(h, p, k):
        at = pl.ds(p * piece, piece)
        return remote(ysum.at[h, at, :], yrecv.at[h, y, at, :], r_send.at[h, p, k - 1],
                      r_recv.at[h, p, k - 1], {"tensor": y_at(k)})

    def bands(p, body):
        def band(i, carry):
            body(pl.ds(pl.multiple_of(p * piece + i * 16, 16), 16))
            return carry

        lax.fori_loop(0, piece // 16, band, 0)

    def y_out(h):
        exchange(h).wait_recv()

        def add(at):
            ysum[h, at, :] = (
                part[h, c, at, :].astype(F32) + rsib[h, at, :].astype(F32)
            ).astype(BF)

        for p in range(parts):
            bands(p, add)
            for k in range(1, n_y):
                ring(h, p, k).start()

    def out_at(h, p):
        at = pl.ds(h * half + p * piece, piece)
        return dx_out.at[at, pl.ds(pl.multiple_of(c * wide, side), wide)]

    def done(h, p):
        return res.at[h, pl.ds(p * piece, piece), :]

    def out_sib(h, p):
        return remote(done(h, p), out_at(h, p), o_send.at[h, p], o_recv.at[h, p], {"tensor": sib})

    def out_own(h, p):
        return pltpu.make_async_copy(done(h, p), out_at(h, p), o_loc.at[h, p])

    def y_in(h):
        def add(at):
            mine = ysum[h, at, :].astype(F32)
            acc = jnp.zeros_like(mine)
            for g in range(n_y):
                acc = acc + jnp.where(y == g, mine, yrecv[h, g, at, :].astype(F32))
            res[h, at, :] = acc.astype(BF)

        for p in range(parts):
            for k in range(1, n_y):
                ring(h, p, k).wait_recv()
            bands(p, add)
            out_sib(h, p).start()
            out_own(h, p).start()

    g_out = (gin_out, gout_out)

    def x_swap(kind, n):
        q = kind * n_c + n
        return remote(stage.at[q, 1 - b], xr.at[q], x_send.at[q], x_recv.at[q], {"dp": xpeer})

    def wgrad(kind, n):
        def make(i):
            s = n * chunk + i
            if kind == 0:
                return dot(tok_t[s], dpre[s], 1, 0)
            row = table[ROW, s]
            return dot(hid_t[s], jnp.concatenate([gcut0[row], gcut1[row]], 0), 1, 0)

        def use(i, g):
            live = table[LIVE, n * chunk + i].astype(F32)
            bins = (jnp.floor(jnp.clip(g, -CLIP, CLIP) * scale) * live).astype(BF)
            for p in range(n_dp):
                stage[kind * n_c + n, p % 2, p // 2, i] = bins[p * span:(p + 1) * span]

        loop_pairs(chunk, make, use)
        x_swap(kind, n).start()

    def z_copy(kind, n, k):
        q = kind * n_c + n
        return remote(zs.at[q, j_at(k)], zr.at[q, k - 1], z_send.at[q, k - 1],
                      z_recv.at[q, k - 1], {"dp": j_at(k) * 2 + b})

    def z_out(kind, n):
        q = kind * n_c + n
        x_swap(kind, n).wait_recv()
        for k in list(range(1, n_j)) + [0]:
            g = j_at(k)
            zs[q, g] = (stage[q, b, g].astype(F32) + xr[q, g].astype(F32)).astype(BF)
            if k:
                z_copy(kind, n, k).start()

    def z_in(kind, n):
        q = kind * n_c + n
        acc = zs[q, j].astype(F32)
        for k in range(1, n_j):
            z_copy(kind, n, k).wait_recv()
            acc = acc + zr[q, k - 1].astype(F32)
        acc = acc * (1.0 / scale)
        for r in range(span):
            g_out[kind][n * chunk:(n + 1) * chunk, r * side:(r + 1) * side] = acc[:, r, :]

    for w in weights:
        w.start()
    for a in range(2):
        for h in range(2):
            own(a, h).start()
    pl.semaphore_wait(barrier, len(peers))
    start_y(0, 0)
    for a in range(2):
        for h in range(2):
            ag_sib(a, h, 0).start()
    tables()
    start_y(0, 1)
    scan[cap] = jnp.zeros(scan.shape[1:], F32)
    rscan[cap] = jnp.zeros(rscan.shape[1:], F32)
    pass_on(0, 0)
    start_y(1, 0)
    for w in weights:
        w.wait()
    settle(0, 0)
    forward(0)
    pass_on(0, 1)
    start_y(1, 1)
    settle(0, 1)
    forward(1)
    pass_on(1, 0)
    settle(1, 0)
    backward(0)
    exchange(0).start()
    y_out(0)
    pass_on(1, 1)
    settle(1, 1)
    for n in range(n_c):
        wgrad(1, n)
    backward(1, lambda: z_out(1, 0))
    exchange(1).start()
    for n in range(n_c):
        wgrad(0, n)
        if n == 0:
            y_out(1)
        if n + 1 < n_c:
            z_out(1, n + 1)
    z_out(0, 0)
    y_in(0)
    for n in range(1, n_c):
        z_out(0, n)
    for n in range(n_c):
        z_in(1, n)
    y_in(1)
    for n in range(n_c):
        z_in(0, n)
    for h in range(2):
        for p in range(parts):
            out_own(h, p).wait()
            out_sib(h, p).wait()
        exchange(h).wait_send()
        for a in range(2):
            for k in range(1, n_y):
                ag_y(a, h, k).wait_send()
            for k in range(n_y):
                ag_sib(a, h, k).wait_send()
        for p in range(parts):
            for k in range(1, n_y):
                ring(h, p, k).wait_send()
    for kind in range(2):
        for n in range(n_c):
            x_swap(kind, n).wait_send()
            for k in range(1, n_j):
                z_copy(kind, n, k).wait_send()


def local(n_dp, n_t, tokens, out_grad, w_in, w_out, block_rows, block_cols):
    tok_count, shard_width = tokens.shape
    cap, side = w_in.shape[0], w_in.shape[1]
    width = shard_width * n_t
    row_count = width // side
    half, wide, span = tok_count // 2, width // 2, side // n_dp
    n_y, n_j = n_t // 2, n_dp // 2
    chunk = 8 if cap % 8 == 0 else cap
    n_q = 2 * (cap // chunk)
    vm, dma = pltpu.VMEM, pltpu.SemaphoreType.DMA
    gathered = vm((n_t, half, shard_width), BF)
    cuts = vm((row_count, half, side), BF)
    blocks = vm((cap, side, side), BF)
    sums = vm((cap + 1, half, side), F32)
    piece = vm((n_q, n_j, chunk, span, side), BF)
    scratch = [
        pltpu.SMEM((6, max(cap, row_count)), I32),
        gathered, gathered, gathered, gathered,
        cuts, cuts, cuts, cuts, blocks, blocks, sums, sums,
        vm((cap, side, tok_count), BF), vm((cap, side, tok_count), BF),
        vm((cap, tok_count, side), F32),
        vm((cap, tok_count, side), BF),
        vm((2, 2, half, wide), BF), vm((2, half, wide), BF), vm((2, half, wide), BF),
        vm((2, n_y, half, wide), BF), vm((2, half, wide), BF),
        vm((n_q, 2, n_j, chunk, span, side), BF), piece, piece,
        vm((n_q, max(n_j - 1, 1), chunk, span, side), BF),
        dma((2, 2, n_y - 1)), dma((2, 2, n_y - 1)), dma((2, 2, n_y)), dma((2, 2, n_y)),
        dma((2, 2)), dma((2,)), dma((2,)), dma((2,)), dma((2, 2, n_y - 1)),
        dma((2, 2, n_y - 1)), dma((2, 2)), dma((2, 2)), dma((2, 2)), dma((n_q,)), dma((n_q,)),
        dma((n_q, n_j - 1)), dma((n_q, n_j - 1)),
    ]
    any_space = pl.BlockSpec(memory_space=pl.ANY)
    smem, vmem = pl.BlockSpec(memory_space=pltpu.SMEM), pl.BlockSpec(memory_space=vm)
    shapes = (vm((tok_count, width), BF),) + (vm((cap, span * side), F32),) * 2
    return pl.pallas_call(
        functools.partial(kernel, n_dp, n_t, chunk),
        out_shape=shapes,
        in_specs=[smem] * 2 + [any_space] * 4,
        out_specs=(any_space, vmem, vmem),
        scratch_shapes=scratch,
        compiler_params=pltpu.CompilerParams(
            collective_id=0, has_side_effects=True, vmem_limit_bytes=56 * 1024 * 1024
        ),
        cost_estimate=pl.CostEstimate(
            flops=10 * cap * tok_count * side * side,
            bytes_accessed=8 * tok_count * width,
            transcendentals=cap * tok_count * side,
        ),
    )(block_rows, block_cols, tokens, out_grad, w_in, w_out)


def solution(mesh):
    in_specs = (
        P("dp", "tensor"),
        P("dp", "tensor"),
        P("tensor", None, None),
        P("tensor", None, None),
        P("tensor", None),
        P("tensor", None),
    )
    out_specs = (P("dp", None), P("tensor", "dp"), P("tensor", "dp"))
    body = functools.partial(local, mesh.shape["dp"], mesh.shape["tensor"])
    return jax.shard_map(body, mesh=mesh, in_specs=in_specs, out_specs=out_specs, check_vma=False)
```

```python
import functools

import jax
import jax.numpy as jnp
from jax import lax
from jax.experimental import pallas as pl
from jax.experimental.pallas import tpu as pltpu
from jax.sharding import PartitionSpec as P

MESH = pl.DeviceIdType.MESH
BF, F32, I32 = jnp.bfloat16, jnp.float32, jnp.int32
CLIP = 4.0
UNROLL = 4
PREV_COL, END_COL, ROW, LIVE, PREV_ROW, LAST = range(6)


def dot(a, b, ca, cb):
    return lax.dot_general(a, b, (((ca,), (cb,)), ((), ())), preferred_element_type=F32)


def loop(count, body):
    def outer(g, carry):
        for u in range(UNROLL):
            body(g * UNROLL + u)
        return carry

    lax.fori_loop(0, count // UNROLL, outer, 0)


def loop_pairs(count, make, use):
    def outer(g, carry):
        at = [g * UNROLL + u for u in range(UNROLL)]
        made = [make(i) for i in at]
        for i, value in zip(at, made):
            use(i, value)
        return carry

    lax.fori_loop(0, count // UNROLL, outer, 0)


def kernel(
    n_dp, n_t, chunk,
    rows, cols, tok_hbm, grad_hbm, win_hbm, wout_hbm,
    dx_out, gin_out, gout_out,
    table, tok0, tok1, grad0, grad1, tcut0, tcut1, gcut0, gcut1, win, wout, scan, rscan,
    tok_t, hid_t, gate, dpre, part, rsib, ysum, yrecv, res, stage, xr, zs, zr,
    ag_send, ag_recv, sib_send, sib_recv, loc, wloc, p_send, p_recv, r_send, r_recv,
    o_send, o_recv, o_loc, x_send, x_recv, z_send, z_recv,
):
    cap, side = win.shape[0], win.shape[1]
    half = tok0.shape[1]
    per = tok0.shape[2] // side
    n_y, n_j, n_c = n_t // 2, n_dp // 2, cap // chunk
    row_count = n_t * per
    span = side // n_dp
    wide = row_count * side // 2
    scale = 4194304.0 / n_dp
    d, t = lax.axis_index("dp"), lax.axis_index("tensor")
    c, y = lax.rem(t, 2), t // 2
    sib = y * 2 + (1 - c)
    b, j = lax.rem(d, 2), d // 2
    xpeer = j * 2 + (1 - b)

    def y_at(k):
        return lax.rem(y + k + n_y, n_y) * 2 + c

    def j_at(k):
        return lax.rem(j + k + n_j, n_j)

    barrier = pltpu.get_barrier_semaphore()
    peers = [{"tensor": sib}, {"dp": xpeer}]
    peers += [{"tensor": y_at(k)} for k in range(1, n_y)]
    peers += [{"dp": j_at(k) * 2 + b} for k in range(1, n_j)]
    for peer in peers:
        pl.semaphore_signal(barrier, inc=1, device_id=peer, device_id_type=MESH)

    def remote(src, dst, ss, rs, peer):
        return pltpu.make_async_remote_copy(
            src_ref=src, dst_ref=dst, send_sem=ss, recv_sem=rs, device_id=peer, device_id_type=MESH
        )

    hbm = (tok_hbm, grad_hbm)
    held = ((tok0, tok1), (grad0, grad1))
    cut = ((tcut0, tcut1), (gcut0, gcut1))

    def shard(a, h):
        return hbm[a].at[pl.ds(h * half, half), :]

    def ag_y(a, h, k):
        return remote(shard(a, h), held[a][h].at[t], ag_send.at[a, h, k - 1],
                      ag_recv.at[a, h, k - 1], {"tensor": y_at(k)})

    def ag_sib(a, h, k):
        src_t = y_at(-k)
        src = shard(a, h) if k == 0 else held[a][h].at[src_t]
        return remote(src, held[a][h].at[src_t], sib_send.at[a, h, k],
                      sib_recv.at[a, h, k], {"tensor": sib})

    def own(a, h):
        return pltpu.make_async_copy(shard(a, h), held[a][h].at[t], loc.at[a, h])

    weights = [pltpu.make_async_copy(win_hbm, win, wloc.at[0]),
               pltpu.make_async_copy(wout_hbm, wout, wloc.at[1])]

    def start_y(a, h):
        for k in range(1, n_y):
            ag_y(a, h, k).start()

    def pass_on(a, h):
        for k in range(1, n_y):
            ag_y(a, h, k).wait_recv()
            ag_sib(a, h, k).start()

    def settle(a, h):
        own(a, h).wait()
        for k in range(n_y):
            ag_sib(a, h, k).wait_recv()

        def split(g, carry):
            for u in range(per):
                cut[a][h][g * per + u] = held[a][h][g, :, u * side:(u + 1) * side]
            return carry

        lax.fori_loop(0, n_t, split, 0)

    def tables():
        for s in range(cap):
            col, row = cols[0, s], rows[0, s]
            prev_col, prev_row, end_col = I32(cap), I32(cap), I32(s)
            for q in range(s):
                prev_col = jnp.where(cols[0, q] == col, q, prev_col)
                prev_row = jnp.where(rows[0, q] == row, q, prev_row)
            for q in range(s + 1, cap):
                end_col = jnp.where(cols[0, q] == col, q, end_col)
            table[PREV_COL, s] = prev_col
            table[PREV_ROW, s] = prev_row
            table[END_COL, s] = end_col
            table[ROW, s] = jnp.maximum(row, 0)
            table[LIVE, s] = jnp.where(row >= 0, 1, 0)

        def of_row(r, carry):
            last = I32(cap)
            for q in range(cap):
                last = jnp.where(rows[0, q] == r, q, last)
            table[LAST, r] = last
            return carry

        lax.fori_loop(0, row_count, of_row, 0)

    def forward(h):
        at = slice(h * half, (h + 1) * half)

        def make(s):
            block = cut[0][h][table[ROW, s]]
            return block.T, dot(block, win[s], 1, 0)

        def use(s, made):
            tok_t[s, :, at] = made[0]
            scan[s] = made[1] + scan[table[PREV_COL, s]]

        loop_pairs(cap, make, use)

        def point(s):
            pre = scan[table[END_COL, s]]
            sigma = 1.0 / (1.0 + jnp.exp(-pre))
            hid_t[s, :, at] = (pre * sigma).astype(BF).T
            gate[s, at, :] = sigma * (1.0 + pre * (1.0 - sigma))

        loop(cap, point)

    def backward(h, between=None):
        at = pl.ds(h * half, half)

        def make(s):
            return dot(cut[1][h][table[ROW, s]], wout[s], 1, 1)

        def use(s, made):
            scan[s] = made + scan[table[PREV_COL, s]]

        loop_pairs(cap, make, use)

        def point(s):
            dpre[s, at, :] = (scan[table[END_COL, s]] * gate[s, at, :]).astype(BF)

        loop(cap, point)
        if between is not None:
            between()

        def make_term(s):
            return dot(dpre[s, at, :], win[s], 1, 1)

        def use_term(s, made):
            rscan[s] = made + rscan[table[PREV_ROW, s]]

        loop_pairs(cap, make_term, use_term)
        for r in range(row_count):
            at_half, off = divmod(r * side, wide)
            part[h, at_half, :, pl.ds(off, side)] = rscan[table[LAST, r]].astype(BF)

    def exchange(h):
        return remote(part.at[h, 1 - c], rsib.at[h], p_send.at[h], p_recv.at[h], {"tensor": sib})

    parts = 2
    piece = half // parts

    def ring(h, p, k):
        at = pl.ds(p * piece, piece)
        return remote(ysum.at[h, at, :], yrecv.at[h, y, at, :], r_send.at[h, p, k - 1],
                      r_recv.at[h, p, k - 1], {"tensor": y_at(k)})

    def bands(p, body):
        def band(i, carry):
            body(pl.ds(pl.multiple_of(p * piece + i * 16, 16), 16))
            return carry

        lax.fori_loop(0, piece // 16, band, 0)

    def y_out(h):
        exchange(h).wait_recv()

        def add(at):
            ysum[h, at, :] = (
                part[h, c, at, :].astype(F32) + rsib[h, at, :].astype(F32)
            ).astype(BF)

        for p in range(parts):
            bands(p, add)
            for k in range(1, n_y):
                ring(h, p, k).start()

    def out_at(h, p):
        at = pl.ds(h * half + p * piece, piece)
        return dx_out.at[at, pl.ds(pl.multiple_of(c * wide, side), wide)]

    def done(h, p):
        return res.at[h, pl.ds(p * piece, piece), :]

    def out_sib(h, p):
        return remote(done(h, p), out_at(h, p), o_send.at[h, p], o_recv.at[h, p], {"tensor": sib})

    def out_own(h, p):
        return pltpu.make_async_copy(done(h, p), out_at(h, p), o_loc.at[h, p])

    def y_in(h):
        def add(at):
            mine = ysum[h, at, :].astype(F32)
            acc = jnp.zeros_like(mine)
            for g in range(n_y):
                acc = acc + jnp.where(y == g, mine, yrecv[h, g, at, :].astype(F32))
            res[h, at, :] = acc.astype(BF)

        for p in range(parts):
            for k in range(1, n_y):
                ring(h, p, k).wait_recv()
            bands(p, add)
            out_sib(h, p).start()
            out_own(h, p).start()

    g_out = (gin_out, gout_out)

    def x_swap(kind, n):
        q = kind * n_c + n
        return remote(stage.at[q, 1 - b], xr.at[q], x_send.at[q], x_recv.at[q], {"dp": xpeer})

    def wgrad(kind, n):
        def make(i):
            s = n * chunk + i
            if kind == 0:
                return dot(tok_t[s], dpre[s], 1, 0)
            row = table[ROW, s]
            return dot(hid_t[s], jnp.concatenate([gcut0[row], gcut1[row]], 0), 1, 0)

        def use(i, g):
            live = table[LIVE, n * chunk + i].astype(F32)
            bins = (jnp.floor(jnp.clip(g, -CLIP, CLIP) * scale) * live).astype(BF)
            for p in range(n_dp):
                stage[kind * n_c + n, p % 2, p // 2, i] = bins[p * span:(p + 1) * span]

        loop_pairs(chunk, make, use)
        x_swap(kind, n).start()

    def z_copy(kind, n, k):
        q = kind * n_c + n
        return remote(zs.at[q, j_at(k)], zr.at[q, k - 1], z_send.at[q, k - 1],
                      z_recv.at[q, k - 1], {"dp": j_at(k) * 2 + b})

    def z_out(kind, n):
        q = kind * n_c + n
        x_swap(kind, n).wait_recv()
        for k in list(range(1, n_j)) + [0]:
            g = j_at(k)
            zs[q, g] = (stage[q, b, g].astype(F32) + xr[q, g].astype(F32)).astype(BF)
            if k:
                z_copy(kind, n, k).start()

    def z_in(kind, n):
        q = kind * n_c + n
        acc = zs[q, j].astype(F32)
        for k in range(1, n_j):
            z_copy(kind, n, k).wait_recv()
            acc = acc + zr[q, k - 1].astype(F32)
        acc = acc * (1.0 / scale)
        for r in range(span):
            g_out[kind][n * chunk:(n + 1) * chunk, r * side:(r + 1) * side] = acc[:, r, :]

    for w in weights:
        w.start()
    for a in range(2):
        for h in range(2):
            own(a, h).start()
    pl.semaphore_wait(barrier, len(peers))
    start_y(0, 0)
    for a in range(2):
        for h in range(2):
            ag_sib(a, h, 0).start()
    tables()
    start_y(0, 1)
    scan[cap] = jnp.zeros(scan.shape[1:], F32)
    rscan[cap] = jnp.zeros(rscan.shape[1:], F32)
    pass_on(0, 0)
    start_y(1, 0)
    for w in weights:
        w.wait()
    settle(0, 0)
    forward(0)
    pass_on(0, 1)
    start_y(1, 1)
    settle(0, 1)
    forward(1)
    pass_on(1, 0)
    settle(1, 0)
    backward(0)
    exchange(0).start()
    y_out(0)
    pass_on(1, 1)
    settle(1, 1)
    for n in range(n_c):
        wgrad(1, n)

    def between():
        for n in range(n_c):
            z_out(1, n)
            wgrad(0, n)

    backward(1, between)
    exchange(1).start()
    z_out(0, 0)
    y_out(1)
    for n in range(1, n_c):
        z_out(0, n)
    y_in(0)
    for n in range(n_c):
        z_in(1, n)
    y_in(1)
    for n in range(n_c):
        z_in(0, n)
    for h in range(2):
        for p in range(parts):
            out_own(h, p).wait()
            out_sib(h, p).wait()
        exchange(h).wait_send()
        for a in range(2):
            for k in range(1, n_y):
                ag_y(a, h, k).wait_send()
            for k in range(n_y):
                ag_sib(a, h, k).wait_send()
        for p in range(parts):
            for k in range(1, n_y):
                ring(h, p, k).wait_send()
    for kind in range(2):
        for n in range(n_c):
            x_swap(kind, n).wait_send()
            for k in range(1, n_j):
                z_copy(kind, n, k).wait_send()


def hand_over(dx, gin, gout, dx_out, gin_out, gout_out, sem):
    pieces = sem.shape[0] - 2
    band = dx.shape[0] // pieces
    at = [pl.ds(i * band, band) for i in range(pieces)]
    legs = [(dx.at[w], dx_out.at[w]) for w in at] + [(gin, gin_out), (gout, gout_out)]
    copies = [pltpu.make_async_copy(a, b, sem.at[i]) for i, (a, b) in enumerate(legs)]
    for copy in copies:
        copy.start()
    for copy in copies:
        copy.wait()


def local(n_dp, n_t, tokens, out_grad, w_in, w_out, block_rows, block_cols):
    tok_count, shard_width = tokens.shape
    cap, side = w_in.shape[0], w_in.shape[1]
    width = shard_width * n_t
    row_count = width // side
    half, wide, span = tok_count // 2, width // 2, side // n_dp
    n_y, n_j = n_t // 2, n_dp // 2
    chunk = 8 if cap % 8 == 0 else cap
    n_q = 2 * (cap // chunk)
    vm, dma = pltpu.VMEM, pltpu.SemaphoreType.DMA
    gathered = vm((n_t, half, shard_width), BF)
    cuts = vm((row_count, half, side), BF)
    blocks = vm((cap, side, side), BF)
    sums = vm((cap + 1, half, side), F32)
    piece = vm((n_q, n_j, chunk, span, side), BF)
    scratch = [
        pltpu.SMEM((6, max(cap, row_count)), I32),
        gathered, gathered, gathered, gathered,
        cuts, cuts, cuts, cuts, blocks, blocks, sums, sums,
        vm((cap, side, tok_count), BF), vm((cap, side, tok_count), BF),
        vm((cap, tok_count, side), F32),
        vm((cap, tok_count, side), BF),
        vm((2, 2, half, wide), BF), vm((2, half, wide), BF), vm((2, half, wide), BF),
        vm((2, n_y, half, wide), BF), vm((2, half, wide), BF),
        vm((n_q, 2, n_j, chunk, span, side), BF), piece, piece,
        vm((n_q, max(n_j - 1, 1), chunk, span, side), BF),
        dma((2, 2, n_y - 1)), dma((2, 2, n_y - 1)), dma((2, 2, n_y)), dma((2, 2, n_y)),
        dma((2, 2)), dma((2,)), dma((2,)), dma((2,)), dma((2, 2, n_y - 1)),
        dma((2, 2, n_y - 1)), dma((2, 2)), dma((2, 2)), dma((2, 2)), dma((n_q,)), dma((n_q,)),
        dma((n_q, n_j - 1)), dma((n_q, n_j - 1)),
    ]
    any_space = pl.BlockSpec(memory_space=pl.ANY)
    smem, vmem = pl.BlockSpec(memory_space=pltpu.SMEM), pl.BlockSpec(memory_space=vm)
    shapes = (vm((tok_count, width), BF),) + (vm((cap, span * side), F32),) * 2
    results = pl.pallas_call(
        functools.partial(kernel, n_dp, n_t, chunk),
        out_shape=shapes,
        in_specs=[smem] * 2 + [any_space] * 4,
        out_specs=(any_space, vmem, vmem),
        scratch_shapes=scratch,
        compiler_params=pltpu.CompilerParams(
            collective_id=0, has_side_effects=True, vmem_limit_bytes=56 * 1024 * 1024
        ),
        cost_estimate=pl.CostEstimate(
            flops=10 * cap * tok_count * side * side,
            bytes_accessed=8 * tok_count * width,
            transcendentals=cap * tok_count * side,
        ),
    )(block_rows, block_cols, tokens, out_grad, w_in, w_out)
    return pl.pallas_call(
        hand_over,
        out_shape=tuple(jax.ShapeDtypeStruct(v.shape, v.dtype) for v in results),
        in_specs=[any_space] * 3,
        out_specs=(any_space,) * 3,
        scratch_shapes=[dma((6,))],
    )(*results)


def solution(mesh):
    in_specs = (
        P("dp", "tensor"),
        P("dp", "tensor"),
        P("tensor", None, None),
        P("tensor", None, None),
        P("tensor", None),
        P("tensor", None),
    )
    out_specs = (P("dp", None), P("tensor", "dp"), P("tensor", "dp"))
    body = functools.partial(local, mesh.shape["dp"], mesh.shape["tensor"])
    return jax.shard_map(body, mesh=mesh, in_specs=in_specs, out_specs=out_specs, check_vma=False)
```

```python
import functools

import jax
import jax.numpy as jnp
from jax import lax
from jax.experimental import pallas as pl
from jax.experimental.pallas import tpu as pltpu
from jax.sharding import PartitionSpec as P

MESH = pl.DeviceIdType.MESH
BF, F32, I32 = jnp.bfloat16, jnp.float32, jnp.int32
CLIP = 4.0
UNROLL = 4
PREV_COL, END_COL, ROW, LIVE, PREV_ROW, LAST = range(6)


def dot(a, b, ca, cb):
    return lax.dot_general(a, b, (((ca,), (cb,)), ((), ())), preferred_element_type=F32)


def loop(count, body):
    def outer(g, carry):
        for u in range(UNROLL):
            body(g * UNROLL + u)
        return carry

    lax.fori_loop(0, count // UNROLL, outer, 0)


def loop_pairs(count, make, use):
    def outer(g, carry):
        at = [g * UNROLL + u for u in range(UNROLL)]
        made = [make(i) for i in at]
        for i, value in zip(at, made):
            use(i, value)
        return carry

    lax.fori_loop(0, count // UNROLL, outer, 0)


def kernel(
    n_dp, n_t, chunk,
    rows, cols, tok_hbm, grad_hbm, win_hbm, wout_hbm,
    dx_out, gin_out, gout_out,
    table, tok0, tok1, grad0, grad1, tcut0, tcut1, gcut0, gcut1, win, wout, scan, rscan,
    tok_t, hid_t, gate, dpre, part, rsib, ysum, yrecv, res, stage, xr, zs, zr,
    ag_send, ag_recv, sib_send, sib_recv, loc, wloc, p_send, p_recv, r_send, r_recv,
    o_send, o_recv, o_loc, x_send, x_recv, z_send, z_recv,
):
    cap, side = win.shape[0], win.shape[1]
    half = tok0.shape[1]
    per = tok0.shape[2] // side
    n_y, n_j, n_c = n_t // 2, n_dp // 2, cap // chunk
    row_count = n_t * per
    span = side // n_dp
    wide = row_count * side // 2
    scale = 4194304.0 / n_dp
    d, t = lax.axis_index("dp"), lax.axis_index("tensor")
    c, y = lax.rem(t, 2), t // 2
    sib = y * 2 + (1 - c)
    b, j = lax.rem(d, 2), d // 2
    xpeer = j * 2 + (1 - b)

    def y_at(k):
        return lax.rem(y + k + n_y, n_y) * 2 + c

    def j_at(k):
        return lax.rem(j + k + n_j, n_j)

    barrier = pltpu.get_barrier_semaphore()
    peers = [{"tensor": sib}, {"dp": xpeer}]
    peers += [{"tensor": y_at(k)} for k in range(1, n_y)]
    peers += [{"dp": j_at(k) * 2 + b} for k in range(1, n_j)]
    for peer in peers:
        pl.semaphore_signal(barrier, inc=1, device_id=peer, device_id_type=MESH)

    def remote(src, dst, ss, rs, peer):
        return pltpu.make_async_remote_copy(
            src_ref=src, dst_ref=dst, send_sem=ss, recv_sem=rs, device_id=peer, device_id_type=MESH
        )

    hbm = (tok_hbm, grad_hbm)
    held = ((tok0, tok1), (grad0, grad1))
    cut = ((tcut0, tcut1), (gcut0, gcut1))

    def shard(a, h):
        return hbm[a].at[pl.ds(h * half, half), :]

    def ag_y(a, h, k):
        return remote(shard(a, h), held[a][h].at[t], ag_send.at[a, h, k - 1],
                      ag_recv.at[a, h, k - 1], {"tensor": y_at(k)})

    def ag_sib(a, h, k):
        src_t = y_at(-k)
        src = shard(a, h) if k == 0 else held[a][h].at[src_t]
        return remote(src, held[a][h].at[src_t], sib_send.at[a, h, k],
                      sib_recv.at[a, h, k], {"tensor": sib})

    def own(a, h):
        return pltpu.make_async_copy(shard(a, h), held[a][h].at[t], loc.at[a, h])

    weights = [pltpu.make_async_copy(win_hbm, win, wloc.at[0]),
               pltpu.make_async_copy(wout_hbm, wout, wloc.at[1])]

    def start_y(a, h):
        for k in range(1, n_y):
            ag_y(a, h, k).start()

    def pass_on(a, h):
        for k in range(1, n_y):
            ag_y(a, h, k).wait_recv()
            ag_sib(a, h, k).start()

    def settle(a, h):
        own(a, h).wait()
        for k in range(n_y):
            ag_sib(a, h, k).wait_recv()

        def split(g, carry):
            for u in range(per):
                cut[a][h][g * per + u] = held[a][h][g, :, u * side:(u + 1) * side]
            return carry

        lax.fori_loop(0, n_t, split, 0)

    def tables():
        for s in range(cap):
            col, row = cols[0, s], rows[0, s]
            prev_col, prev_row, end_col = I32(cap), I32(cap), I32(s)
            for q in range(s):
                prev_col = jnp.where(cols[0, q] == col, q, prev_col)
                prev_row = jnp.where(rows[0, q] == row, q, prev_row)
            for q in range(s + 1, cap):
                end_col = jnp.where(cols[0, q] == col, q, end_col)
            table[PREV_COL, s] = prev_col
            table[PREV_ROW, s] = prev_row
            table[END_COL, s] = end_col
            table[ROW, s] = jnp.maximum(row, 0)
            table[LIVE, s] = jnp.where(row >= 0, 1, 0)

        def of_row(r, carry):
            last = I32(cap)
            for q in range(cap):
                last = jnp.where(rows[0, q] == r, q, last)
            table[LAST, r] = last
            return carry

        lax.fori_loop(0, row_count, of_row, 0)

    def forward(h):
        at = slice(h * half, (h + 1) * half)

        def make(s):
            block = cut[0][h][table[ROW, s]]
            return block.T, dot(block, win[s], 1, 0)

        def use(s, made):
            tok_t[s, :, at] = made[0]
            scan[s] = made[1] + scan[table[PREV_COL, s]]

        loop_pairs(cap, make, use)

        def point(s):
            pre = scan[table[END_COL, s]]
            sigma = 1.0 / (1.0 + jnp.exp(-pre))
            hid_t[s, :, at] = (pre * sigma).astype(BF).T
            gate[s, at, :] = sigma * (1.0 + pre * (1.0 - sigma))

        loop(cap, point)

    def backward(h):
        at = pl.ds(h * half, half)

        def make(s):
            return dot(cut[1][h][table[ROW, s]], wout[s], 1, 1)

        def use(s, made):
            scan[s] = made + scan[table[PREV_COL, s]]

        loop_pairs(cap, make, use)

        def point(s):
            dpre[s, at, :] = (scan[table[END_COL, s]] * gate[s, at, :]).astype(BF)

        loop(cap, point)
        def make_term(s):
            return dot(dpre[s, at, :], win[s], 1, 1)

        def use_term(s, made):
            rscan[s] = made + rscan[table[PREV_ROW, s]]

        loop_pairs(cap, make_term, use_term)
        for r in range(row_count):
            at_half, off = divmod(r * side, wide)
            part[h, at_half, :, pl.ds(off, side)] = rscan[table[LAST, r]].astype(BF)

    def exchange(h):
        return remote(part.at[h, 1 - c], rsib.at[h], p_send.at[h], p_recv.at[h], {"tensor": sib})

    parts = 2
    piece = half // parts

    def ring(h, p, k):
        at = pl.ds(p * piece, piece)
        return remote(ysum.at[h, at, :], yrecv.at[h, y, at, :], r_send.at[h, p, k - 1],
                      r_recv.at[h, p, k - 1], {"tensor": y_at(k)})

    def bands(p, body):
        def band(i, carry):
            body(pl.ds(pl.multiple_of(p * piece + i * 16, 16), 16))
            return carry

        lax.fori_loop(0, piece // 16, band, 0)

    def y_out(h):
        exchange(h).wait_recv()

        def add(at):
            ysum[h, at, :] = (
                part[h, c, at, :].astype(F32) + rsib[h, at, :].astype(F32)
            ).astype(BF)

        for p in range(parts):
            bands(p, add)
            for k in range(1, n_y):
                ring(h, p, k).start()

    def out_at(h, p):
        at = pl.ds(h * half + p * piece, piece)
        return dx_out.at[at, pl.ds(pl.multiple_of(c * wide, side), wide)]

    def done(h, p):
        return res.at[h, pl.ds(p * piece, piece), :]

    def out_sib(h, p):
        return remote(done(h, p), out_at(h, p), o_send.at[h, p], o_recv.at[h, p], {"tensor": sib})

    def out_own(h, p):
        return pltpu.make_async_copy(done(h, p), out_at(h, p), o_loc.at[h, p])

    def y_in(h):
        def add(at):
            mine = ysum[h, at, :].astype(F32)
            acc = jnp.zeros_like(mine)
            for g in range(n_y):
                acc = acc + jnp.where(y == g, mine, yrecv[h, g, at, :].astype(F32))
            res[h, at, :] = acc.astype(BF)

        for p in range(parts):
            for k in range(1, n_y):
                ring(h, p, k).wait_recv()
            bands(p, add)
            out_sib(h, p).start()
            out_own(h, p).start()

    g_out = (gin_out, gout_out)

    def x_swap(kind, n):
        q = kind * n_c + n
        return remote(stage.at[q, 1 - b], xr.at[q], x_send.at[q], x_recv.at[q], {"dp": xpeer})

    def wgrad(kind, n):
        def make(i):
            s = n * chunk + i
            if kind == 0:
                return dot(tok_t[s], dpre[s], 1, 0)
            row = table[ROW, s]
            return dot(hid_t[s], jnp.concatenate([gcut0[row], gcut1[row]], 0), 1, 0)

        def use(i, g):
            live = table[LIVE, n * chunk + i].astype(F32)
            bins = (jnp.floor(jnp.clip(g, -CLIP, CLIP) * scale) * live).astype(BF)
            for p in range(n_dp):
                stage[kind * n_c + n, p % 2, p // 2, i] = bins[p * span:(p + 1) * span]

        loop_pairs(chunk, make, use)
        x_swap(kind, n).start()

    def z_copy(kind, n, k):
        q = kind * n_c + n
        return remote(zs.at[q, j_at(k)], zr.at[q, k - 1], z_send.at[q, k - 1],
                      z_recv.at[q, k - 1], {"dp": j_at(k) * 2 + b})

    def z_out(kind, n):
        q = kind * n_c + n
        x_swap(kind, n).wait_recv()
        for k in list(range(1, n_j)) + [0]:
            g = j_at(k)
            zs[q, g] = (stage[q, b, g].astype(F32) + xr[q, g].astype(F32)).astype(BF)
            if k:
                z_copy(kind, n, k).start()

    def z_in(kind, n):
        q = kind * n_c + n
        acc = zs[q, j].astype(F32)
        for k in range(1, n_j):
            z_copy(kind, n, k).wait_recv()
            acc = acc + zr[q, k - 1].astype(F32)
        acc = acc * (1.0 / scale)
        for r in range(span):
            g_out[kind][n * chunk:(n + 1) * chunk, r * side:(r + 1) * side] = acc[:, r, :]

    for w in weights:
        w.start()
    for a in range(2):
        for h in range(2):
            own(a, h).start()
    pl.semaphore_wait(barrier, len(peers))
    start_y(0, 0)
    for a in range(2):
        for h in range(2):
            ag_sib(a, h, 0).start()
    tables()
    start_y(0, 1)
    scan[cap] = jnp.zeros(scan.shape[1:], F32)
    rscan[cap] = jnp.zeros(rscan.shape[1:], F32)
    pass_on(0, 0)
    start_y(1, 0)
    for w in weights:
        w.wait()
    settle(0, 0)
    forward(0)
    pass_on(0, 1)
    start_y(1, 1)
    settle(0, 1)
    forward(1)
    pass_on(1, 0)
    settle(1, 0)
    backward(0)
    exchange(0).start()
    y_out(0)
    pass_on(1, 1)
    settle(1, 1)
    backward(1)
    exchange(1).start()
    wgrad(1, 0)
    y_out(1)
    for n in range(1, n_c):
        wgrad(1, n)
    for n in range(n_c):
        z_out(1, n)
        wgrad(0, n)
    for n in range(n_c):
        z_out(0, n)
    y_in(0)
    for n in range(n_c):
        z_in(1, n)
    y_in(1)
    for n in range(n_c):
        z_in(0, n)
    for h in range(2):
        for p in range(parts):
            out_own(h, p).wait()
            out_sib(h, p).wait()
        exchange(h).wait_send()
        for a in range(2):
            for k in range(1, n_y):
                ag_y(a, h, k).wait_send()
            for k in range(n_y):
                ag_sib(a, h, k).wait_send()
        for p in range(parts):
            for k in range(1, n_y):
                ring(h, p, k).wait_send()
    for kind in range(2):
        for n in range(n_c):
            x_swap(kind, n).wait_send()
            for k in range(1, n_j):
                z_copy(kind, n, k).wait_send()


def hand_over(dx, gin, gout, dx_out, gin_out, gout_out, sem):
    pieces = sem.shape[0] - 2
    band = dx.shape[0] // pieces
    at = [pl.ds(i * band, band) for i in range(pieces)]
    legs = [(dx.at[w], dx_out.at[w]) for w in at] + [(gin, gin_out), (gout, gout_out)]
    copies = [pltpu.make_async_copy(a, b, sem.at[i]) for i, (a, b) in enumerate(legs)]
    for copy in copies:
        copy.start()
    for copy in copies:
        copy.wait()


def local(n_dp, n_t, tokens, out_grad, w_in, w_out, block_rows, block_cols):
    tok_count, shard_width = tokens.shape
    cap, side = w_in.shape[0], w_in.shape[1]
    width = shard_width * n_t
    row_count = width // side
    half, wide, span = tok_count // 2, width // 2, side // n_dp
    n_y, n_j = n_t // 2, n_dp // 2
    chunk = 8 if cap % 8 == 0 else cap
    n_q = 2 * (cap // chunk)
    vm, dma = pltpu.VMEM, pltpu.SemaphoreType.DMA
    gathered = vm((n_t, half, shard_width), BF)
    cuts = vm((row_count, half, side), BF)
    blocks = vm((cap, side, side), BF)
    sums = vm((cap + 1, half, side), F32)
    piece = vm((n_q, n_j, chunk, span, side), BF)
    scratch = [
        pltpu.SMEM((6, max(cap, row_count)), I32),
        gathered, gathered, gathered, gathered,
        cuts, cuts, cuts, cuts, blocks, blocks, sums, sums,
        vm((cap, side, tok_count), BF), vm((cap, side, tok_count), BF),
        vm((cap, tok_count, side), F32),
        vm((cap, tok_count, side), BF),
        vm((2, 2, half, wide), BF), vm((2, half, wide), BF), vm((2, half, wide), BF),
        vm((2, n_y, half, wide), BF), vm((2, half, wide), BF),
        vm((n_q, 2, n_j, chunk, span, side), BF), piece, piece,
        vm((n_q, max(n_j - 1, 1), chunk, span, side), BF),
        dma((2, 2, n_y - 1)), dma((2, 2, n_y - 1)), dma((2, 2, n_y)), dma((2, 2, n_y)),
        dma((2, 2)), dma((2,)), dma((2,)), dma((2,)), dma((2, 2, n_y - 1)),
        dma((2, 2, n_y - 1)), dma((2, 2)), dma((2, 2)), dma((2, 2)), dma((n_q,)), dma((n_q,)),
        dma((n_q, n_j - 1)), dma((n_q, n_j - 1)),
    ]
    any_space = pl.BlockSpec(memory_space=pl.ANY)
    smem, vmem = pl.BlockSpec(memory_space=pltpu.SMEM), pl.BlockSpec(memory_space=vm)
    shapes = (vm((tok_count, width), BF),) + (vm((cap, span * side), F32),) * 2
    results = pl.pallas_call(
        functools.partial(kernel, n_dp, n_t, chunk),
        out_shape=shapes,
        in_specs=[smem] * 2 + [any_space] * 4,
        out_specs=(any_space, vmem, vmem),
        scratch_shapes=scratch,
        compiler_params=pltpu.CompilerParams(
            collective_id=0, has_side_effects=True, vmem_limit_bytes=56 * 1024 * 1024
        ),
        cost_estimate=pl.CostEstimate(
            flops=10 * cap * tok_count * side * side,
            bytes_accessed=8 * tok_count * width,
            transcendentals=cap * tok_count * side,
        ),
    )(block_rows, block_cols, tokens, out_grad, w_in, w_out)
    return pl.pallas_call(
        hand_over,
        out_shape=tuple(jax.ShapeDtypeStruct(v.shape, v.dtype) for v in results),
        in_specs=[any_space] * 3,
        out_specs=(any_space,) * 3,
        scratch_shapes=[dma((6,))],
        compiler_params=pltpu.CompilerParams(vmem_limit_bytes=4 * 1024 * 1024),
    )(*results)


def solution(mesh):
    in_specs = (
        P("dp", "tensor"),
        P("dp", "tensor"),
        P("tensor", None, None),
        P("tensor", None, None),
        P("tensor", None),
        P("tensor", None),
    )
    out_specs = (P("dp", None), P("tensor", "dp"), P("tensor", "dp"))
    body = functools.partial(local, mesh.shape["dp"], mesh.shape["tensor"])
    return jax.shard_map(body, mesh=mesh, in_specs=in_specs, out_specs=out_specs, check_vma=False)
```

```python
import functools

import jax
import jax.numpy as jnp
from jax import lax
from jax.experimental import pallas as pl
from jax.experimental.pallas import tpu as pltpu
from jax.sharding import PartitionSpec as P

MESH = pl.DeviceIdType.MESH
BF, F32, I32 = jnp.bfloat16, jnp.float32, jnp.int32
CLIP = 4.0
UNROLL, AHEAD = 8, 4
PREV_COL, END_COL, ROW, LIVE, PREV_ROW, LAST = range(6)


def dot(a, b, ca, cb):
    return lax.dot_general(a, b, (((ca,), (cb,)), ((), ())), preferred_element_type=F32)


def loop(count, body):
    def outer(g, carry):
        for u in range(UNROLL):
            body(g * UNROLL + u)
        return carry

    lax.fori_loop(0, count // UNROLL, outer, 0)


def loop_pairs(count, make, use):
    def outer(g, carry):
        at = [g * UNROLL + u for u in range(UNROLL)]
        made = [make(i) for i in at[:AHEAD]]
        for n, i in enumerate(at):
            use(i, made[n])
            if n + AHEAD < UNROLL:
                made.append(make(at[n + AHEAD]))
        return carry

    lax.fori_loop(0, count // UNROLL, outer, 0)


def kernel(
    n_dp, n_t, chunk,
    rows, cols, tok_hbm, grad_hbm, win_hbm, wout_hbm,
    dx_out, gin_out, gout_out,
    table, tok0, tok1, grad0, grad1, tcut0, tcut1, gcut0, gcut1, win, wout, scan, rscan,
    tok_t, hid_t, gate, dpre, part, rsib, ysum, yrecv, res, stage, xr, zs, zr,
    ag_send, ag_recv, sib_send, sib_recv, loc, wloc, p_send, p_recv, r_send, r_recv,
    o_send, o_recv, o_loc, x_send, x_recv, z_send, z_recv,
):
    cap, side = win.shape[0], win.shape[1]
    half = tok0.shape[1]
    per = tok0.shape[2] // side
    n_y, n_j, n_c = n_t // 2, n_dp // 2, cap // chunk
    row_count = n_t * per
    span = side // n_dp
    wide = row_count * side // 2
    scale = 4194304.0 / n_dp
    d, t = lax.axis_index("dp"), lax.axis_index("tensor")
    c, y = lax.rem(t, 2), t // 2
    sib = y * 2 + (1 - c)
    b, j = lax.rem(d, 2), d // 2
    xpeer = j * 2 + (1 - b)

    def y_at(k):
        return lax.rem(y + k + n_y, n_y) * 2 + c

    def j_at(k):
        return lax.rem(j + k + n_j, n_j)

    barrier = pltpu.get_barrier_semaphore()
    peers = [{"tensor": sib}, {"dp": xpeer}]
    peers += [{"tensor": y_at(k)} for k in range(1, n_y)]
    peers += [{"dp": j_at(k) * 2 + b} for k in range(1, n_j)]
    for peer in peers:
        pl.semaphore_signal(barrier, inc=1, device_id=peer, device_id_type=MESH)

    def remote(src, dst, ss, rs, peer):
        return pltpu.make_async_remote_copy(
            src_ref=src, dst_ref=dst, send_sem=ss, recv_sem=rs, device_id=peer, device_id_type=MESH
        )

    hbm = (tok_hbm, grad_hbm)
    held = ((tok0, tok1), (grad0, grad1))
    cut = ((tcut0, tcut1), (gcut0, gcut1))

    def shard(a, h):
        return hbm[a].at[pl.ds(h * half, half), :]

    def ag_y(a, h, k):
        return remote(shard(a, h), held[a][h].at[t], ag_send.at[a, h, k - 1],
                      ag_recv.at[a, h, k - 1], {"tensor": y_at(k)})

    def ag_sib(a, h, k):
        src_t = y_at(-k)
        src = shard(a, h) if k == 0 else held[a][h].at[src_t]
        return remote(src, held[a][h].at[src_t], sib_send.at[a, h, k],
                      sib_recv.at[a, h, k], {"tensor": sib})

    def own(a, h):
        return pltpu.make_async_copy(shard(a, h), held[a][h].at[t], loc.at[a, h])

    weights = [pltpu.make_async_copy(win_hbm, win, wloc.at[0]),
               pltpu.make_async_copy(wout_hbm, wout, wloc.at[1])]

    def start_y(a, h):
        for k in range(1, n_y):
            ag_y(a, h, k).start()

    def pass_on(a, h):
        for k in range(1, n_y):
            ag_y(a, h, k).wait_recv()
            ag_sib(a, h, k).start()

    def settle(a, h):
        own(a, h).wait()
        for k in range(n_y):
            ag_sib(a, h, k).wait_recv()

        def split(g, carry):
            for u in range(per):
                cut[a][h][g * per + u] = held[a][h][g, :, u * side:(u + 1) * side]
            return carry

        lax.fori_loop(0, n_t, split, 0)

    def tables():
        for s in range(cap):
            col, row = cols[0, s], rows[0, s]
            prev_col, prev_row, end_col = I32(cap), I32(cap), I32(s)
            for q in range(s):
                prev_col = jnp.where(cols[0, q] == col, q, prev_col)
                prev_row = jnp.where(rows[0, q] == row, q, prev_row)
            for q in range(s + 1, cap):
                end_col = jnp.where(cols[0, q] == col, q, end_col)
            table[PREV_COL, s] = prev_col
            table[PREV_ROW, s] = prev_row
            table[END_COL, s] = end_col
            table[ROW, s] = jnp.maximum(row, 0)
            table[LIVE, s] = jnp.where(row >= 0, 1, 0)

        def of_row(r, carry):
            last = I32(cap)
            for q in range(cap):
                last = jnp.where(rows[0, q] == r, q, last)
            table[LAST, r] = last
            return carry

        lax.fori_loop(0, row_count, of_row, 0)

    def forward(h):
        at = slice(h * half, (h + 1) * half)

        def make(s):
            block = cut[0][h][table[ROW, s]]
            return block.T, dot(block, win[s], 1, 0)

        def use(s, made):
            tok_t[s, :, at] = made[0]
            scan[s] = made[1] + scan[table[PREV_COL, s]]

        loop_pairs(cap, make, use)

        def point(s):
            pre = scan[table[END_COL, s]]
            sigma = 1.0 / (1.0 + jnp.exp(-pre))
            hid_t[s, :, at] = (pre * sigma).astype(BF).T
            gate[s, at, :] = sigma * (1.0 + pre * (1.0 - sigma))

        loop(cap, point)

    def backward(h, between=None):
        at = pl.ds(h * half, half)

        def make(s):
            return dot(cut[1][h][table[ROW, s]], wout[s], 1, 1)

        def use(s, made):
            scan[s] = made + scan[table[PREV_COL, s]]

        loop_pairs(cap, make, use)

        def point(s):
            dpre[s, at, :] = (scan[table[END_COL, s]] * gate[s, at, :]).astype(BF)

        loop(cap, point)
        if between is not None:
            between()

        def make_term(s):
            return dot(dpre[s, at, :], win[s], 1, 1)

        def use_term(s, made):
            rscan[s] = made + rscan[table[PREV_ROW, s]]

        loop_pairs(cap, make_term, use_term)
        for r in range(row_count):
            at_half, off = divmod(r * side, wide)
            part[h, at_half, :, pl.ds(off, side)] = rscan[table[LAST, r]].astype(BF)

    def exchange(h):
        return remote(part.at[h, 1 - c], rsib.at[h], p_send.at[h], p_recv.at[h], {"tensor": sib})

    parts = 2
    piece = half // parts

    def ring(h, p, k):
        at = pl.ds(p * piece, piece)
        return remote(ysum.at[h, at, :], yrecv.at[h, y, at, :], r_send.at[h, p, k - 1],
                      r_recv.at[h, p, k - 1], {"tensor": y_at(k)})

    def bands(p, body):
        def band(i, carry):
            body(pl.ds(pl.multiple_of(p * piece + i * 16, 16), 16))
            return carry

        lax.fori_loop(0, piece // 16, band, 0)

    def y_out(h):
        exchange(h).wait_recv()

        def add(at):
            ysum[h, at, :] = (
                part[h, c, at, :].astype(F32) + rsib[h, at, :].astype(F32)
            ).astype(BF)

        for p in range(parts):
            bands(p, add)
            for k in range(1, n_y):
                ring(h, p, k).start()

    def out_at(h, p):
        at = pl.ds(h * half + p * piece, piece)
        return dx_out.at[at, pl.ds(pl.multiple_of(c * wide, side), wide)]

    def done(h, p):
        return res.at[h, pl.ds(p * piece, piece), :]

    def out_sib(h, p):
        return remote(done(h, p), out_at(h, p), o_send.at[h, p], o_recv.at[h, p], {"tensor": sib})

    def out_own(h, p):
        return pltpu.make_async_copy(done(h, p), out_at(h, p), o_loc.at[h, p])

    def y_in(h):
        def add(at):
            mine = ysum[h, at, :].astype(F32)
            acc = jnp.zeros_like(mine)
            for g in range(n_y):
                acc = acc + jnp.where(y == g, mine, yrecv[h, g, at, :].astype(F32))
            res[h, at, :] = acc.astype(BF)

        for p in range(parts):
            for k in range(1, n_y):
                ring(h, p, k).wait_recv()
            bands(p, add)
            out_sib(h, p).start()
            out_own(h, p).start()

    g_out = (gin_out, gout_out)

    def x_swap(kind, n):
        q = kind * n_c + n
        return remote(stage.at[q, 1 - b], xr.at[q], x_send.at[q], x_recv.at[q], {"dp": xpeer})

    def wgrad(kind, n):
        def make(i):
            s = n * chunk + i
            if kind == 0:
                return dot(tok_t[s], dpre[s], 1, 0)
            row = table[ROW, s]
            return dot(hid_t[s], jnp.concatenate([gcut0[row], gcut1[row]], 0), 1, 0)

        def use(i, g):
            live = table[LIVE, n * chunk + i].astype(F32)
            bins = (jnp.floor(jnp.clip(g, -CLIP, CLIP) * scale) * live).astype(BF)
            for p in range(n_dp):
                stage[kind * n_c + n, p % 2, p // 2, i] = bins[p * span:(p + 1) * span]

        loop_pairs(chunk, make, use)
        x_swap(kind, n).start()

    def z_copy(kind, n, k):
        q = kind * n_c + n
        return remote(zs.at[q, j_at(k)], zr.at[q, k - 1], z_send.at[q, k - 1],
                      z_recv.at[q, k - 1], {"dp": j_at(k) * 2 + b})

    def z_out(kind, n):
        q = kind * n_c + n
        x_swap(kind, n).wait_recv()
        for k in list(range(1, n_j)) + [0]:
            g = j_at(k)
            zs[q, g] = (stage[q, b, g].astype(F32) + xr[q, g].astype(F32)).astype(BF)
            if k:
                z_copy(kind, n, k).start()

    def z_in(kind, n):
        q = kind * n_c + n
        acc = zs[q, j].astype(F32)
        for k in range(1, n_j):
            z_copy(kind, n, k).wait_recv()
            acc = acc + zr[q, k - 1].astype(F32)
        acc = acc * (1.0 / scale)
        for r in range(span):
            g_out[kind][n * chunk:(n + 1) * chunk, r * side:(r + 1) * side] = acc[:, r, :]

    for w in weights:
        w.start()
    for a in range(2):
        for h in range(2):
            own(a, h).start()
    pl.semaphore_wait(barrier, len(peers))
    start_y(0, 0)
    for a in range(2):
        for h in range(2):
            ag_sib(a, h, 0).start()
    tables()
    start_y(0, 1)
    scan[cap] = jnp.zeros(scan.shape[1:], F32)
    rscan[cap] = jnp.zeros(rscan.shape[1:], F32)
    pass_on(0, 0)
    start_y(1, 0)
    for w in weights:
        w.wait()
    settle(0, 0)
    forward(0)
    pass_on(0, 1)
    start_y(1, 1)
    settle(0, 1)
    forward(1)
    pass_on(1, 0)
    settle(1, 0)
    backward(0)
    exchange(0).start()
    y_out(0)
    pass_on(1, 1)
    settle(1, 1)
    for n in range(n_c):
        wgrad(1, n)
    backward(1, lambda: z_out(1, 0))
    exchange(1).start()
    for n in range(n_c):
        wgrad(0, n)
        if n == 0:
            y_out(1)
        if n + 1 < n_c:
            z_out(1, n + 1)
    z_out(0, 0)
    y_in(0)
    for n in range(1, n_c):
        z_out(0, n)
    for n in range(n_c):
        z_in(1, n)
    y_in(1)
    for n in range(n_c):
        z_in(0, n)
    for h in range(2):
        for p in range(parts):
            out_own(h, p).wait()
            out_sib(h, p).wait()
        exchange(h).wait_send()
        for a in range(2):
            for k in range(1, n_y):
                ag_y(a, h, k).wait_send()
            for k in range(n_y):
                ag_sib(a, h, k).wait_send()
        for p in range(parts):
            for k in range(1, n_y):
                ring(h, p, k).wait_send()
    for kind in range(2):
        for n in range(n_c):
            x_swap(kind, n).wait_send()
            for k in range(1, n_j):
                z_copy(kind, n, k).wait_send()


def hand_over(dx, gin, gout, dx_out, gin_out, gout_out, sem):
    pieces = sem.shape[0] - 2
    band = dx.shape[0] // pieces
    at = [pl.ds(i * band, band) for i in range(pieces)]
    legs = [(dx.at[w], dx_out.at[w]) for w in at] + [(gin, gin_out), (gout, gout_out)]
    copies = [pltpu.make_async_copy(a, b, sem.at[i]) for i, (a, b) in enumerate(legs)]
    for copy in copies:
        copy.start()
    for copy in copies:
        copy.wait()


def local(n_dp, n_t, tokens, out_grad, w_in, w_out, block_rows, block_cols):
    tok_count, shard_width = tokens.shape
    cap, side = w_in.shape[0], w_in.shape[1]
    width = shard_width * n_t
    row_count = width // side
    half, wide, span = tok_count // 2, width // 2, side // n_dp
    n_y, n_j = n_t // 2, n_dp // 2
    chunk = 8 if cap % 8 == 0 else cap
    n_q = 2 * (cap // chunk)
    vm, dma = pltpu.VMEM, pltpu.SemaphoreType.DMA
    gathered = vm((n_t, half, shard_width), BF)
    cuts = vm((row_count, half, side), BF)
    blocks = vm((cap, side, side), BF)
    sums = vm((cap + 1, half, side), F32)
    piece = vm((n_q, n_j, chunk, span, side), BF)
    scratch = [
        pltpu.SMEM((6, max(cap, row_count)), I32),
        gathered, gathered, gathered, gathered,
        cuts, cuts, cuts, cuts, blocks, blocks, sums, sums,
        vm((cap, side, tok_count), BF), vm((cap, side, tok_count), BF),
        vm((cap, tok_count, side), F32),
        vm((cap, tok_count, side), BF),
        vm((2, 2, half, wide), BF), vm((2, half, wide), BF), vm((2, half, wide), BF),
        vm((2, n_y, half, wide), BF), vm((2, half, wide), BF),
        vm((n_q, 2, n_j, chunk, span, side), BF), piece, piece,
        vm((n_q, max(n_j - 1, 1), chunk, span, side), BF),
        dma((2, 2, n_y - 1)), dma((2, 2, n_y - 1)), dma((2, 2, n_y)), dma((2, 2, n_y)),
        dma((2, 2)), dma((2,)), dma((2,)), dma((2,)), dma((2, 2, n_y - 1)),
        dma((2, 2, n_y - 1)), dma((2, 2)), dma((2, 2)), dma((2, 2)), dma((n_q,)), dma((n_q,)),
        dma((n_q, n_j - 1)), dma((n_q, n_j - 1)),
    ]
    any_space = pl.BlockSpec(memory_space=pl.ANY)
    smem, vmem = pl.BlockSpec(memory_space=pltpu.SMEM), pl.BlockSpec(memory_space=vm)
    shapes = (vm((tok_count, width), BF),) + (vm((cap, span * side), F32),) * 2
    results = pl.pallas_call(
        functools.partial(kernel, n_dp, n_t, chunk),
        out_shape=shapes,
        in_specs=[smem] * 2 + [any_space] * 4,
        out_specs=(any_space, vmem, vmem),
        scratch_shapes=scratch,
        compiler_params=pltpu.CompilerParams(
            collective_id=0, has_side_effects=True, vmem_limit_bytes=56 * 1024 * 1024
        ),
        cost_estimate=pl.CostEstimate(
            flops=10 * cap * tok_count * side * side,
            bytes_accessed=8 * tok_count * width,
            transcendentals=cap * tok_count * side,
        ),
    )(block_rows, block_cols, tokens, out_grad, w_in, w_out)
    return pl.pallas_call(
        hand_over,
        out_shape=tuple(jax.ShapeDtypeStruct(v.shape, v.dtype) for v in results),
        in_specs=[any_space] * 3,
        out_specs=(any_space,) * 3,
        scratch_shapes=[dma((6,))],
        compiler_params=pltpu.CompilerParams(vmem_limit_bytes=4 * 1024 * 1024),
    )(*results)


def solution(mesh):
    in_specs = (
        P("dp", "tensor"),
        P("dp", "tensor"),
        P("tensor", None, None),
        P("tensor", None, None),
        P("tensor", None),
        P("tensor", None),
    )
    out_specs = (P("dp", None), P("tensor", "dp"), P("tensor", "dp"))
    body = functools.partial(local, mesh.shape["dp"], mesh.shape["tensor"])
    return jax.shard_map(body, mesh=mesh, in_specs=in_specs, out_specs=out_specs, check_vma=False)
```
